32 devices in a mesh: space: 8 (over z, x), rep: 4 (over y, core).
Axes of the slice: x: 2, y: 2, z: 4, core: 2. Of those that a mesh axis runs over, the one named last changes fastest.
Arguments:
- voxels: bfloat16 [4, 32, 512, 128], P('rep', 'space'), may hold values from -6 to 6
- occupied: int32 [4, 32], P('rep', 'space'), may hold values from 0 to 1, as said below
- neighbours: int32 [4, 32, 6], P('rep', 'space'), may hold values from -1 to 31, as said below
- first_weight: bfloat16 [27, 128, 128], replicated, may hold values from -0.109375 to 0.109375
- second_weight: bfloat16 [27, 128, 128], replicated, may hold values from -0.109375 to 0.109375
- cotangent: bfloat16 [4, 32, 512, 128], P('rep', 'space'), may hold values from -0.0234375 to 0.0234375
Outputs:
- output_field: bfloat16 [4, 32, 512, 128], P('rep', 'space')
- first_grad: float32 [27, 128, 128], replicated
- second_grad: float32 [27, 128, 128], replicated
The draws below stay inside these ranges and needn't reach their ends.
Inputs may be any that keep to these rules, and one draw needn't show every extreme that they name: In every slab each device of space holds n blocks in its first n slots (occupied 1) and padding after them, n from 1 to 4; in some slab the last device holds 4. `neighbours`: device s of space owns one tile of 2 x 2 x 1 block positions. With h = log2(8) - 1, bit h of s is the tile's third coordinate (the slab is two tiles deep in the third dimension), and below it bit 2k of s is bit k of the tile's first coordinate and bit 2k+1 of s bit k of its second. Entry f names owner * 4 + slot of the occupied block of the same slab across face f (-x, +x, -y, +y, -z, +z), or -1 where there is none or the slot is padding; if a names b across face f, b names a across the opposite face.
All inputs are finite; a program needn't handle non-finite values.
Results may differ from the reference program's by a relative error of at most 0.0031.
Values may be sent and summed in bfloat16 or wider, within the bound.
A program may use at most 128 MiB of HBM per device.

```python
import jax
import jax.numpy as jnp
from jax import lax

C = 128
EDGE = 8
DEPTH = 1
BLK = 4
VOX = 512
OWNERS = 8
REPS = 4
SLOTS = 32


def morton_owner(column, row_pos, layer, bit_total):
    plane_bits = bit_total - 1
    wide_bits = (plane_bits + 1) // 2
    tall_bits = plane_bits // 2
    owner = layer * 2 ** plane_bits
    for bit_place in range(wide_bits):
        owner = owner + column // 2 ** bit_place % 2 * 4 ** bit_place
    for bit_place in range(tall_bits):
        owner = owner + row_pos // 2 ** bit_place % 2 * (2 * 4 ** bit_place)
    return owner


def slab_layout(key):
    base = jax.random.fold_in(key, 17)
    count_key, order_key, full_key = jax.random.split(base, 3)
    counts = jax.random.randint(count_key, (REPS, OWNERS), BLK // 4, BLK + 1)
    full_slab = jax.random.randint(full_key, (), 0, REPS)
    slab_ids = jnp.arange(REPS)[:, None]
    owner_ids = jnp.arange(OWNERS)[None, :]
    counts = jnp.where((slab_ids == full_slab) & (owner_ids == OWNERS - 1), BLK, counts).astype(jnp.int32)
    order_keys = jax.random.split(order_key, REPS * OWNERS)
    placed = jax.vmap(lambda single: jax.random.permutation(single, BLK))(order_keys)
    placed = placed.reshape(REPS, OWNERS, BLK).astype(jnp.int32)
    matches = placed[:, :, :, None] == jnp.arange(BLK)[None, None, None, :]
    slot_of = jnp.sum(matches.astype(jnp.int32) * jnp.arange(BLK, dtype=jnp.int32)[None, None, :, None], axis=2)
    flat_slots = slot_of.reshape(REPS, OWNERS * BLK)
    bit_total = int(OWNERS).bit_length() - 1
    plane_bits = bit_total - 1
    wide_bits = (plane_bits + 1) // 2
    tall_bits = plane_bits // 2
    owner_vec = jnp.arange(OWNERS, dtype=jnp.int32)
    tile_column = jnp.zeros_like(owner_vec)
    tile_row = jnp.zeros_like(owner_vec)
    for bit_place in range(wide_bits):
        tile_column = tile_column + owner_vec // 2 ** (2 * bit_place) % 2 * 2 ** bit_place
    for bit_place in range(tall_bits):
        tile_row = tile_row + owner_vec // 2 ** (2 * bit_place + 1) % 2 * 2 ** bit_place
    tile_layer = owner_vec // 2 ** plane_bits
    columns_total = 2 * 2 ** wide_bits
    rows_total = 2 * 2 ** tall_bits
    layers_total = 2 * DEPTH
    across = placed // (2 * DEPTH)
    along = placed // DEPTH % 2
    height = placed % DEPTH
    global_x = 2 * tile_column[None, :, None] + across
    global_y = 2 * tile_row[None, :, None] + along
    global_z = DEPTH * tile_layer[None, :, None] + height
    occupied_self = jnp.arange(BLK)[None, None, :] < counts[:, :, None]
    links = []
    for step_x, step_y, step_z in ((-1, 0, 0), (1, 0, 0), (0, -1, 0), (0, 1, 0), (0, 0, -1), (0, 0, 1)):
        next_x = global_x + step_x
        next_y = global_y + step_y
        next_z = global_z + step_z
        inside = (next_x >= 0) & (next_x < columns_total) & (next_y >= 0) & (next_y < rows_total) & (next_z >= 0) & (next_z < layers_total)
        next_x = jnp.clip(next_x, 0, columns_total - 1)
        next_y = jnp.clip(next_y, 0, rows_total - 1)
        next_z = jnp.clip(next_z, 0, layers_total - 1)
        owner_next = morton_owner(next_x // 2, next_y // 2, next_z // DEPTH, bit_total)
        position_next = (next_x % 2 * 2 + next_y % 2) * DEPTH + next_z % DEPTH
        slot_next = jnp.take_along_axis(flat_slots, (owner_next * BLK + position_next).reshape(REPS, -1), axis=1)
        slot_next = slot_next.reshape(REPS, OWNERS, BLK)
        count_next = jnp.take_along_axis(counts, owner_next.reshape(REPS, -1), axis=1).reshape(REPS, OWNERS, BLK)
        alive = inside & occupied_self & (slot_next < count_next)
        links.append(jnp.where(alive, owner_next * BLK + slot_next, -1))
    neighbour_table = jnp.stack(links, axis=-1).reshape(REPS, SLOTS, 6).astype(jnp.int32)
    occupancy = occupied_self.astype(jnp.int32).reshape(REPS, SLOTS)
    return (occupancy, neighbour_table)


def draw_occupied(key, part):
    return slab_layout(key)[0]


def draw_neighbours(key, part):
    return slab_layout(key)[1]


def level_of(rng, shape, cuts, least, top_value):
    level, own = 1.0, jax.random.fold_in(rng, 6)
    for dim, blocks in cuts:
        heights = jnp.exp(jax.random.uniform(jax.random.fold_in(own, dim), (blocks,), jnp.float32, least / len(cuts), top_value / len(cuts)))
        level = level * jnp.repeat(heights, shape[dim] // blocks).reshape([-1 if axis == dim else 1 for axis in range(len(shape))])
    return level


def centred(rng, extent, scale, reach, shards=(), kind=jnp.bfloat16):
    factor_of = level_of(rng, extent, shards, -0.22, 0.18) if shards else 1.0
    drawn = jax.random.normal(rng, extent, jnp.float32) * scale * factor_of
    return jnp.minimum(jnp.maximum(drawn, -reach), reach).astype(kind)


def setup_inputs(seed: int = 0) -> dict:
    key_of = jax.random.split(jax.random.key(seed), 7)
    voxels = centred(key_of[0], (REPS, SLOTS, VOX, C), 1.0, 6.0, ((0, 4), (1, 8)))
    occupied = draw_occupied(jax.random.fold_in(key_of[6], 71), 0)
    neighbours = draw_neighbours(jax.random.fold_in(key_of[6], 71), 0)
    first_weight = centred(key_of[3], (27, C, C), (27 * C) ** -0.5, 0.109375)
    second_weight = centred(key_of[4], (27, C, C), (27 * C) ** -0.5, 0.109375)
    cotangent = centred(key_of[5], (REPS, SLOTS, VOX, C), ((REPS * SLOTS * VOX) ** -0.5), 0.0234375, ((0, 4), (1, 8)))
    return dict(voxels=voxels, occupied=occupied, neighbours=neighbours, first_weight=first_weight, second_weight=second_weight, cotangent=cotangent)


OPPOSITE_FACES = (1, 0, 3, 2, 5, 4)


def face_layers(blocks):
    return jnp.stack([blocks[:, 0], blocks[:, -1], blocks[:, :, 0], blocks[:, :, -1], blocks[:, :, :, 0], blocks[:, :, :, -1]], axis=1)


def assemble(blocks, faces):
    padded = jnp.pad(blocks, ((0, 0), (1, 1), (1, 1), (1, 1), (0, 0)))
    padded = padded.at[:, 0, 1:-1, 1:-1].set(faces[:, 0])
    padded = padded.at[:, -1, 1:-1, 1:-1].set(faces[:, 1])
    padded = padded.at[:, 1:-1, 0, 1:-1].set(faces[:, 2])
    padded = padded.at[:, 1:-1, -1, 1:-1].set(faces[:, 3])
    padded = padded.at[:, 1:-1, 1:-1, 0].set(faces[:, 4])
    padded = padded.at[:, 1:-1, 1:-1, -1].set(faces[:, 5])
    return padded


def gather_faces(blocks, links):
    slot_count = blocks.shape[0]
    layers = face_layers(blocks).reshape(slot_count * 6, EDGE, EDGE, C)
    valid = links >= 0
    opposite = jnp.array(OPPOSITE_FACES, jnp.int32)
    rows = jnp.where(valid, links * 6 + opposite[None, :], 0).astype(jnp.int32)
    return layers[rows] * valid.astype(blocks.dtype)[:, :, None, None, None]


def tap_group(padded, first_tap, backward):
    columns = []
    for second_tap in range(3):
        for third_tap in range(3):
            if backward:
                starts = (2 - first_tap, 2 - second_tap, 2 - third_tap)
            else:
                starts = (first_tap, second_tap, third_tap)
            piece = padded[:, starts[0]:starts[0] + EDGE, starts[1]:starts[1] + EDGE, starts[2]:starts[2] + EDGE]
            columns.append(piece.reshape(-1, C))
    return jnp.concatenate(columns, axis=1)


def convolve(padded, weights):
    total = jnp.zeros((padded.shape[0] * VOX, C), jnp.float32)
    for first_tap in range(3):
        group = tap_group(padded, first_tap, False)
        stacked = weights[first_tap * 9:(first_tap + 1) * 9].reshape(9 * C, C)
        total = total + jnp.dot(group, stacked, preferred_element_type=jnp.float32)
    return total


def convolve_back(padded, weights):
    total = jnp.zeros((padded.shape[0] * VOX, C), jnp.float32)
    for first_tap in range(3):
        group = tap_group(padded, first_tap, True)
        stacked = jnp.swapaxes(weights[first_tap * 9:(first_tap + 1) * 9], 1, 2).reshape(9 * C, C)
        total = total + jnp.dot(group, stacked, preferred_element_type=jnp.float32)
    return total


def weight_terms(padded, grads):
    parts = []
    for first_tap in range(3):
        group = tap_group(padded, first_tap, False)
        part = lax.dot_general(group, grads, (((0,), (0,)), ((), ())), preferred_element_type=jnp.float32)
        parts.append(part.reshape(9, C, C))
    return jnp.concatenate(parts, axis=0)


def reference(voxels, occupied, neighbours, first_weight, second_weight, cotangent):
    def one_slab(items):
        field, flags, links, incoming = items
        keep = flags.astype(jnp.bfloat16)[:, None, None]
        masked = field * keep
        voxel_mask = jnp.repeat(flags.astype(jnp.float32), VOX)[:, None]
        blocks = masked.reshape(-1, EDGE, EDGE, EDGE, C)
        input_padded = assemble(blocks, gather_faces(blocks, links))
        first = convolve(input_padded, first_weight)
        hidden = (jax.nn.silu(first) * voxel_mask).astype(jnp.bfloat16)
        hidden_blocks = hidden.reshape(-1, EDGE, EDGE, EDGE, C)
        hidden_padded = assemble(hidden_blocks, gather_faces(hidden_blocks, links))
        second = convolve(hidden_padded, second_weight)
        output = ((masked.reshape(-1, C).astype(jnp.float32) + second) * voxel_mask).astype(jnp.bfloat16)
        grad_out = (incoming * keep).reshape(-1, C)
        second_terms = weight_terms(hidden_padded, grad_out)
        grad_blocks = grad_out.reshape(-1, EDGE, EDGE, EDGE, C)
        grad_padded = assemble(grad_blocks, gather_faces(grad_blocks, links))
        grad_hidden = convolve_back(grad_padded, second_weight)
        sigma = jax.nn.sigmoid(first)
        grad_first = (grad_hidden * sigma * (1.0 + first * (1.0 - sigma)) * voxel_mask).astype(jnp.bfloat16)
        first_terms = weight_terms(input_padded, grad_first)
        return output.reshape(-1, VOX, C), first_terms, second_terms

    output_field, first_terms, second_terms = lax.map(one_slab, (voxels, occupied, neighbours, cotangent))
    return output_field, jnp.sum(first_terms, axis=0), jnp.sum(second_terms, axis=0)
```

```python
import functools

import jax
import jax.numpy as jnp
from jax import lax
from jax.experimental import pallas as pl
from jax.experimental.pallas import tpu as pltpu
from jax.sharding import PartitionSpec as P

MESH = pl.DeviceIdType.MESH
OPP = (1, 0, 3, 2, 5, 4)
F32 = jnp.float32
BF16 = jnp.bfloat16


def spread(number, start):
    return [(2 * place + start, place) for place in range(number)]


def tile_place(device, spaces):
    plane = spaces.bit_length() - 2
    wide, tall = (plane + 1) // 2, plane // 2
    column = sum(device // 2**src % 2 * 2**dst for src, dst in spread(wide, 0))
    row = sum(device // 2**src % 2 * 2**dst for src, dst in spread(tall, 1))
    layer = device // 2**plane
    return column, row, layer


def tile_owner(column, row, layer, spaces):
    plane = spaces.bit_length() - 2
    wide, tall = (plane + 1) // 2, plane // 2
    owner = layer * 2**plane
    owner = owner + sum(column // 2**dst % 2 * 2**src for src, dst in spread(wide, 0))
    return owner + sum(row // 2**dst % 2 * 2**src for src, dst in spread(tall, 1))


def tile_neighbours(device, spaces):
    plane = spaces.bit_length() - 2
    sizes = (2 ** ((plane + 1) // 2), 2 ** (plane // 2), 2)
    place = tile_place(device, spaces)
    found = []
    for face in range(6):
        dim, step = face // 2, 1 if face % 2 else -1
        moved = list(place)
        moved[dim] = (moved[dim] + step + sizes[dim]) % sizes[dim]
        there = place[dim] < sizes[dim] - 1 if face % 2 else place[dim] > 0
        found.append((there, tile_owner(*moved, spaces)))
    return found


def kernel(
    spaces, reps, reduce_here,
    occ, links, vox, w1, w2, cot,
    out, g1, g2,
    T, U, FB0, FB1, FB2, VX, VH, VG, WA, WB, WC, FI, GA, GB, R, A0, B0, XY, S1, B1, ZR,
    face_send, face_recv, red_send, red_recv,
):
    FB = (FB0, FB1, FB2)
    space, rep = lax.axis_index("space"), lax.axis_index("rep")
    near = tile_neighbours(space, spaces)
    x, z, y, core = space % 2, space // 2, rep // 2, rep % 2

    def core_peer():
        return (space, y * 2 + (1 - core))

    def xy_peer(d):
        flipped_x = 1 - x if d & 1 else x
        flipped_y = 1 - y if d & 2 else y
        return (z * 2 + flipped_x, flipped_y * 2 + core)

    def z_far(d):
        low = 1 - z % 2 if d & 1 else z % 2
        high = 1 - z // 2 if d & 2 else z // 2
        return high * 2 + low

    def z_peer(d):
        return (z_far(d) * 2 + x, rep)

    barrier = pltpu.get_barrier_semaphore()
    if reduce_here:
        peers = [core_peer()] + [xy_peer(d) for d in (1, 2, 3)] + [z_peer(d) for d in (1, 2, 3)]
        for peer in peers:
            pl.semaphore_signal(barrier, inc=1, device_id=peer, device_id_type=MESH)
        pl.semaphore_wait(barrier, 7)
    else:
        total = 0
        for there, owner in near:
            total = total + there.astype(jnp.int32)

            @pl.when(there)
            def _():
                pl.semaphore_signal(barrier, inc=1, device_id=(owner, rep), device_id_type=MESH)

        pl.semaphore_wait(barrier, total)

    def face_copy(field, face):
        return pltpu.make_async_remote_copy(
            src_ref=FB[field].at[OPP[face], pl.ds(0, 4)],
            dst_ref=FB[field].at[OPP[face], pl.ds(4, 4)],
            send_sem=face_send.at[field, face],
            recv_sem=face_recv.at[field, OPP[face]],
            device_id=(near[face][1], rep),
            device_id_type=MESH,
        )

    def arrival(field, face):
        return pltpu.make_async_remote_copy(
            src_ref=FB[field].at[face, pl.ds(0, 4)],
            dst_ref=FB[field].at[face, pl.ds(4, 4)],
            send_sem=face_send.at[field, face],
            recv_sem=face_recv.at[field, face],
            device_id=(near[face][1], rep),
            device_id_type=MESH,
        )

    def send_faces(field):
        for s in range(4):
            cube = T[field, s].reshape(8, 8, 8, 128)
            parts = (
                cube[0].reshape(64, 128), cube[7].reshape(64, 128),
                cube[:, 0].reshape(64, 128), cube[:, 7].reshape(64, 128),
                T[field, s, pl.ds(0, 64, stride=8), :], T[field, s, pl.ds(7, 64, stride=8), :],
            )
            for face, part in enumerate(parts):
                FB[field][OPP[face], s] = part.astype(BF16)
        for face in (4, 5, 2, 3, 0, 1):
            @pl.when(near[face][0])
            def _():
                face_copy(field, face).start()

    def wait_faces(field):
        for face in range(6):
            @pl.when(near[face][0])
            def _():
                arrival(field, face).wait_recv()

    def drain_faces(field):
        for face in range(6):
            @pl.when(near[face][0])
            def _():
                face_copy(field, face).wait_send()

    def halo(field, face, s):
        link = links[s * 6 + face]
        there = link >= 0
        safe = jnp.where(there, link, 0)
        index = safe % 4 + jnp.where(safe // 4 == space, 0, 4)
        index = jnp.where(there, index, 0)
        got = FB[field][face, index].astype(F32)
        return jnp.where(there, got, 0.0)

    level = lax.broadcasted_iota(jnp.int32, (1, 8, 128), 1)

    def down(cube):
        return pltpu.roll(cube, 1, 1)

    def up(cube):
        return pltpu.roll(cube, 7, 1)

    def put_centre(field, V):
        def body(i, carry):
            rows = [T[field, s, pl.ds(pl.multiple_of(i * 64, 64), 64), :].reshape(8, 8, 128) for s in range(4)]
            V[i + 1, 1:9, :, 128:256] = jnp.concatenate(rows, axis=1).astype(BF16)
            return carry

        lax.fori_loop(0, 8, body, 0)

    def put_halos(field, V):
        zero = jnp.zeros((32, 384), BF16)
        for i in (0, 9):
            for j in (0, 9):
                V[i, j] = zero
        for s in range(4):
            cube = T[field, s].reshape(64, 8, 128)
            U[0, s] = down(cube).reshape(512, 128)
            U[1, s] = up(cube).reshape(512, 128)
            U[0, s, pl.ds(0, 64, stride=8), :] = halo(field, 4, s)
            U[1, s, pl.ds(7, 64, stride=8), :] = halo(field, 5, s)

        def body(i, carry):
            for n, lane in ((0, 0), (1, 256)):
                rows = [U[n, s, pl.ds(pl.multiple_of(i * 64, 64), 64), :].reshape(8, 8, 128) for s in range(4)]
                V[i + 1, 1:9, :, lane:lane + 128] = jnp.concatenate(rows, axis=1).astype(BF16)
            return carry

        lax.fori_loop(0, 8, body, 0)
        for face in range(4):
            layers = [halo(field, face, s).reshape(8, 8, 128) for s in range(4)]
            lower = [jnp.where(level == 0, 0.0, down(layer)) for layer in layers]
            upper = [jnp.where(level == 7, 0.0, up(layer)) for layer in layers]
            for lane, group in ((0, lower), (128, layers), (256, upper)):
                value = jnp.concatenate(group, axis=1).astype(BF16)
                edge = 9 if face % 2 else 0
                if face < 2:
                    V[edge, 1:9, :, lane:lane + 128] = value
                else:
                    V[1:9, edge, :, lane:lane + 128] = value

    def convolve(V, W, emit):
        def body(half, carry):
            groups = []
            for p in range(2):
                base = half * 4 + p * 2
                groups.append(jnp.concatenate(
                    [V[base + a, dj:dj + 8].reshape(256, 384) for a in range(4) for dj in range(3)], axis=1
                ))
            both = jnp.concatenate(groups, axis=0)
            total = jnp.dot(both, W[...], preferred_element_type=F32)
            for p in range(2):
                for h in range(2):
                    emit(half * 4 + p * 2 + h, total[p * 256:p * 256 + 256, h * 128:h * 128 + 128])
            return carry

        lax.fori_loop(0, 2, body, 0)

    def weight_product(G, V, which):
        columns = [(dj, dk) for dj in range(3) for dk in range(3)]
        for first in range(0, 9, 2):
            part = columns[first:first + 2]
            right = jnp.concatenate(
                [V[:, dj:dj + 8, :, dk * 128:dk * 128 + 128].reshape(2560, 128) for dj, dk in part], axis=1
            )
            R[which, :, first * 128:(first + len(part)) * 128] = jnp.dot(
                G[...], right, preferred_element_type=F32
            )

    def put_turned(G, i, rows):
        turned = rows.T.astype(BF16)
        for di in range(3):
            at = pl.multiple_of((i + di) * 256, 256)
            G[di * 128:di * 128 + 128, pl.ds(at, 256)] = turned

    def clear_turned(G):
        for di in range(3):
            for i in range(10):
                if not 0 <= i - di < 8:
                    G[di * 128:di * 128 + 128, i * 256:i * 256 + 256] = jnp.zeros((128, 256), BF16)

    def widen(W, source):
        blank = jnp.zeros((1152, 128), BF16)
        for a in range(4):
            W[a * 1152:a * 1152 + 1152, 0:128] = source[a] if a < 3 else blank
            W[a * 1152:a * 1152 + 1152, 128:256] = source[a - 1] if a > 0 else blank

    def widen_back(W, source):
        blank = jnp.zeros((1152, 128), BF16)
        W[3456:4608, 0:128] = blank
        W[0:1152, 128:256] = blank
        for a in range(3):
            for t in range(9):
                turned = source[2 - a, (8 - t) * 128:(8 - t) * 128 + 128, :].T
                W[a * 1152 + t * 128:a * 1152 + t * 128 + 128, 0:128] = turned
                W[(a + 1) * 1152 + t * 128:(a + 1) * 1152 + t * 128 + 128, 128:256] = turned

    def red_copy(which, slot, src, dst, peer):
        return pltpu.make_async_remote_copy(
            src_ref=src, dst_ref=dst, send_sem=red_send.at[which, slot],
            recv_sem=red_recv.at[which, slot], device_id=peer, device_id_type=MESH,
        )

    outs = (g1, g2)
    quarter = y * 2 + x
    my_row = pl.multiple_of(core * 192 + quarter * 48, 16)

    def quarter_of(d):
        return (1 - y if d & 2 else y) * 2 + (1 - x if d & 1 else x)

    def core_copy(w):
        other = pl.multiple_of((1 - core) * 192, 16)
        return red_copy(w, 0, R.at[w, pl.ds(other, 192)], A0.at[w], core_peer())

    def xy_copy(w, d):
        row = pl.multiple_of(quarter_of(d) * 48, 16)
        return red_copy(w, d, B0.at[w, pl.ds(row, 48)], XY.at[w, d - 1], xy_peer(d))

    def z_copy(w, d):
        lane = pl.multiple_of(z_far(d) * 256, 128)
        return red_copy(w, 3 + d, B1.at[w, :, pl.ds(lane, 384)], ZR.at[w, d - 1], z_peer(d))

    def z_back(w, d):
        ref = outs[w].at[pl.ds(my_row, 48), pl.ds(pl.multiple_of(z * 256, 128), 256)]
        return red_copy(w, 6 + d, ref, ref, z_peer(d))

    def z_from(w, d):
        ref = outs[w].at[pl.ds(my_row, 48), pl.ds(pl.multiple_of(z_far(d) * 256, 128), 256)]
        return red_copy(w, 6 + d, ref, ref, z_peer(d))

    def z_last(w, d):
        ref = outs[w].at[pl.ds(my_row, 48), pl.ds(1024, 128)]
        return red_copy(w, 9 + d, ref, ref, z_peer(d))

    def xy_back(w, d, mine):
        q = quarter if mine else quarter_of(d)
        ref = outs[w].at[pl.ds(pl.multiple_of(core * 192 + q * 48, 16), 48)]
        return red_copy(w, 12 + d, ref, ref, xy_peer(d))

    def core_back(w, mine):
        c = core if mine else 1 - core
        ref = outs[w].at[pl.ds(pl.multiple_of(c * 192, 16), 192)]
        return red_copy(w, 16, ref, ref, core_peer())

    D = (1, 2, 3)

    def red_start(w):
        core_copy(w).start()

    def red_xy(w):
        core_copy(w).wait()
        mine = pl.multiple_of(core * 192, 16)
        summed = R[w, pl.ds(mine, 192), :] + A0[w]
        R[w, pl.ds(mine, 192), :] = summed
        B0[w] = summed.astype(BF16)
        for d in (3, 1, 2):
            xy_copy(w, d).start()

    def red_z(w):
        for d in D:
            xy_copy(w, d).wait()
        summed = R[w, pl.ds(my_row, 48), :]
        for d in D:
            summed = summed + XY[w, d - 1].astype(F32)
        S1[w] = summed
        B1[w] = summed.astype(BF16)
        for d in (3, 2, 1):
            z_copy(w, d).start()

    def red_back_z(w):
        for d in D:
            z_copy(w, d).wait()
        summed = S1[w, :, pl.ds(pl.multiple_of(z * 256, 128), 384)]
        for d in D:
            summed = summed + ZR[w, d - 1].astype(F32)
        summed = summed.astype(BF16)
        outs[w][pl.ds(my_row, 48), pl.ds(pl.multiple_of(z * 256, 128), 256)] = summed[:, 0:256]
        for d in (3, 2, 1):
            z_back(w, d).start()

        @pl.when(z == 3)
        def _():
            outs[w][pl.ds(my_row, 48), pl.ds(1024, 128)] = summed[:, 256:384]
            for d in D:
                z_last(w, d).start()

    def red_back_xy(w):
        for d in D:
            z_from(w, d).wait_recv()
            @pl.when(z_far(d) == 3)
            def _():
                z_last(w, d).wait_recv()
        for d in (3, 1, 2):
            xy_back(w, d, True).start()

    def red_back_core(w):
        for d in D:
            xy_back(w, d, False).wait_recv()
        core_back(w, True).start()

    def red_end(w):
        core_back(w, False).wait_recv()
        core_back(w, True).wait_send()
        for d in D:
            xy_back(w, d, True).wait_send()
            z_back(w, d).wait_send()

        @pl.when(z == 3)
        def _():
            for d in D:
                z_last(w, d).wait_send()

    keep = [occ[s].astype(F32) for s in range(4)]
    slot_of = lax.broadcasted_iota(jnp.int32, (32, 128), 0) // 8
    mask = jnp.zeros((32, 128), F32)
    for s in range(4):
        mask = jnp.where(slot_of == s, keep[s], mask)
    mask = mask[None]

    def load(field, source):
        for s in range(4):
            T[field, s] = source[s].astype(F32) * keep[s]

    def masked_rows(rows):
        return (rows.reshape(8, 32, 128) * mask)

    load(0, vox)
    send_faces(0)
    load(1, cot)
    send_faces(1)
    put_centre(0, VX)
    put_centre(1, VG)
    widen(WA, w1)
    widen_back(WB, w2)
    widen(WC, w2)
    clear_turned(GA)
    clear_turned(GB)

    def turn_out(i, carry):
        put_turned(GB, i, VG[i + 1, 1:9, :, 128:256].reshape(256, 128).astype(F32))
        return carry

    lax.fori_loop(0, 8, turn_out, 0)
    wait_faces(0)
    put_halos(0, VX)

    def emit_first(i, rows):
        FI[i] = rows
        hidden = masked_rows(rows * jax.nn.sigmoid(rows))
        for s in range(4):
            T[2, s, pl.ds(pl.multiple_of(i * 64, 64), 64), :] = hidden[:, s * 8:s * 8 + 8].reshape(64, 128)

    convolve(VX, WA, emit_first)
    send_faces(2)
    wait_faces(1)
    put_halos(1, VG)

    def emit_grad(i, rows):
        first = FI[i]
        sigma = jax.nn.sigmoid(first)
        grad = masked_rows(rows * sigma * (1.0 + first * (1.0 - sigma))).reshape(256, 128)
        put_turned(GA, i, grad)

    convolve(VG, WB, emit_grad)
    weight_product(GA, VX, 0)
    if reduce_here:
        red_start(0)
    put_centre(2, VH)
    wait_faces(2)
    put_halos(2, VH)
    if reduce_here:
        red_xy(0)
    weight_product(GB, VH, 1)
    if reduce_here:
        red_start(1)
        red_z(0)

    def emit_out(i, rows):
        inner = VX[i + 1, 1:9, :, 128:256].astype(F32) + rows.reshape(8, 32, 128)
        inner = (inner * mask).astype(BF16).astype(F32)
        for s in range(4):
            out[s, pl.ds(pl.multiple_of(i * 64, 64), 64), :] = inner[:, s * 8:s * 8 + 8].reshape(64, 128).astype(BF16)

    if reduce_here:
        red_xy(1)
        red_back_z(0)
    convolve(VH, WC, emit_out)
    if reduce_here:
        red_z(1)
        red_back_xy(0)
        red_back_z(1)
        red_back_core(0)
        red_back_xy(1)
        red_end(0)
        red_back_core(1)
        red_end(1)
    else:
        g1[...] = R[0]
        g2[...] = R[1]
    for field in range(3):
        drain_faces(field)


def solution(mesh):
    spaces, reps = mesh.shape["space"], mesh.shape["rep"]
    reduce_here = spaces == 8 and reps == 4
    grad_type = BF16 if reduce_here else F32

    def local(voxels, occupied, neighbours, first_weight, second_weight, cotangent):
        smem = pl.BlockSpec(memory_space=pltpu.SMEM)
        vmem = pl.BlockSpec(memory_space=pltpu.VMEM)
        out, first, second = pl.pallas_call(
            functools.partial(kernel, spaces, reps, reduce_here),
            out_shape=(
                jax.ShapeDtypeStruct((4, 512, 128), BF16),
                jax.ShapeDtypeStruct((384, 1152), grad_type),
                jax.ShapeDtypeStruct((384, 1152), grad_type),
            ),
            in_specs=[smem, smem, vmem, vmem, vmem, vmem],
            out_specs=(vmem, vmem, vmem),
            scratch_shapes=[
                pltpu.VMEM((3, 4, 512, 128), F32),
                pltpu.VMEM((2, 4, 512, 128), F32),
                pltpu.VMEM((6, 8, 64, 128), BF16),
                pltpu.VMEM((6, 8, 64, 128), BF16),
                pltpu.VMEM((6, 8, 64, 128), BF16),
                pltpu.VMEM((10, 10, 32, 384), BF16),
                pltpu.VMEM((10, 10, 32, 384), BF16),
                pltpu.VMEM((10, 10, 32, 384), BF16),
                pltpu.VMEM((4608, 256), BF16),
                pltpu.VMEM((4608, 256), BF16),
                pltpu.VMEM((4608, 256), BF16),
                pltpu.VMEM((8, 256, 128), F32),
                pltpu.VMEM((384, 2560), BF16),
                pltpu.VMEM((384, 2560), BF16),
                pltpu.VMEM((2, 384, 1152), F32),
                pltpu.VMEM((2, 192, 1152), F32),
                pltpu.VMEM((2, 192, 1152), BF16),
                pltpu.VMEM((2, 3, 48, 1152), BF16),
                pltpu.VMEM((2, 48, 1152), F32),
                pltpu.VMEM((2, 48, 1152), BF16),
                pltpu.VMEM((2, 3, 48, 384), BF16),
                pltpu.SemaphoreType.DMA((3, 6)),
                pltpu.SemaphoreType.DMA((3, 6)),
                pltpu.SemaphoreType.DMA((2, 17)),
                pltpu.SemaphoreType.DMA((2, 17)),
            ],
            compiler_params=pltpu.CompilerParams(
                collective_id=0, has_side_effects=True, vmem_limit_bytes=56 * 2**20
            ),
            cost_estimate=pl.CostEstimate(flops=9_060_000_000, bytes_accessed=6_000_000, transcendentals=500_000),
        )(
            occupied.reshape(4), neighbours.reshape(24), voxels.reshape(4, 512, 128),
            first_weight.reshape(3, 1152, 128), second_weight.reshape(3, 1152, 128),
            cotangent.reshape(4, 512, 128),
        )
        if not reduce_here:
            first, second = lax.psum((first, second), ("space", "rep"))

        def turned(grad):
            grad = grad.reshape(3, 128, 9, 128).transpose(0, 2, 3, 1)
            return grad.reshape(27, 128, 128).astype(F32)

        return out[None], turned(first), turned(second)

    placed = (
        P("rep", "space", None, None),
        P("rep", "space"),
        P("rep", "space", None),
        P(),
        P(),
        P("rep", "space", None, None),
    )
    return jax.shard_map(
        local,
        mesh=mesh,
        in_specs=placed,
        out_specs=(P("rep", "space", None, None), P(), P()),
        check_vma=False,
    )
```

```python
import functools

import jax
import jax.numpy as jnp
from jax import lax
from jax.experimental import pallas as pl
from jax.experimental.pallas import tpu as pltpu
from jax.sharding import PartitionSpec as P

MESH = pl.DeviceIdType.MESH
OPP = (1, 0, 3, 2, 5, 4)
F32 = jnp.float32
BF16 = jnp.bfloat16


def spread(number, start):
    return [(2 * place + start, place) for place in range(number)]


def tile_place(device, spaces):
    plane = spaces.bit_length() - 2
    wide, tall = (plane + 1) // 2, plane // 2
    column = sum(device // 2**src % 2 * 2**dst for src, dst in spread(wide, 0))
    row = sum(device // 2**src % 2 * 2**dst for src, dst in spread(tall, 1))
    layer = device // 2**plane
    return column, row, layer


def tile_owner(column, row, layer, spaces):
    plane = spaces.bit_length() - 2
    wide, tall = (plane + 1) // 2, plane // 2
    owner = layer * 2**plane
    owner = owner + sum(column // 2**dst % 2 * 2**src for src, dst in spread(wide, 0))
    return owner + sum(row // 2**dst % 2 * 2**src for src, dst in spread(tall, 1))


def tile_neighbours(device, spaces):
    plane = spaces.bit_length() - 2
    sizes = (2 ** ((plane + 1) // 2), 2 ** (plane // 2), 2)
    place = tile_place(device, spaces)
    found = []
    for face in range(6):
        dim, step = face // 2, 1 if face % 2 else -1
        moved = list(place)
        moved[dim] = (moved[dim] + step + sizes[dim]) % sizes[dim]
        there = place[dim] < sizes[dim] - 1 if face % 2 else place[dim] > 0
        found.append((there, tile_owner(*moved, spaces)))
    return found


def kernel(
    spaces, reps, reduce_here,
    occ, links, vox, w1, w2, cot,
    out, g1, g2,
    T, U, FB0, FB1, FB2, VX, VH, VG, WA, WB, WC, FI, GA, GB, R, A0, B0, XY, S1, B1, ZR, F0, F1,
    face_send, face_recv, red_send, red_recv,
):
    FB = (FB0, FB1, FB2)
    space, rep = lax.axis_index("space"), lax.axis_index("rep")
    near = tile_neighbours(space, spaces)
    x, z, y, core = space % 2, space // 2, rep // 2, rep % 2

    def core_peer():
        return (space, y * 2 + (1 - core))

    def xy_peer(d):
        flipped_x = 1 - x if d & 1 else x
        flipped_y = 1 - y if d & 2 else y
        return (z * 2 + flipped_x, flipped_y * 2 + core)

    def z_far(d):
        low = 1 - z % 2 if d & 1 else z % 2
        high = 1 - z // 2 if d & 2 else z // 2
        return high * 2 + low

    def z_peer(d):
        return (z_far(d) * 2 + x, rep)

    barrier = pltpu.get_barrier_semaphore()
    if reduce_here:
        peers = [core_peer()] + [xy_peer(d) for d in (1, 2, 3)] + [z_peer(d) for d in (1, 2, 3)]
        for peer in peers:
            pl.semaphore_signal(barrier, inc=1, device_id=peer, device_id_type=MESH)
        pl.semaphore_wait(barrier, 7)
    else:
        total = 0
        for there, owner in near:
            total = total + there.astype(jnp.int32)

            @pl.when(there)
            def _():
                pl.semaphore_signal(barrier, inc=1, device_id=(owner, rep), device_id_type=MESH)

        pl.semaphore_wait(barrier, total)

    def face_copy(field, face):
        return pltpu.make_async_remote_copy(
            src_ref=FB[field].at[OPP[face], pl.ds(0, 4)],
            dst_ref=FB[field].at[OPP[face], pl.ds(4, 4)],
            send_sem=face_send.at[field, face],
            recv_sem=face_recv.at[field, OPP[face]],
            device_id=(near[face][1], rep),
            device_id_type=MESH,
        )

    def arrival(field, face):
        return pltpu.make_async_remote_copy(
            src_ref=FB[field].at[face, pl.ds(0, 4)],
            dst_ref=FB[field].at[face, pl.ds(4, 4)],
            send_sem=face_send.at[field, face],
            recv_sem=face_recv.at[field, face],
            device_id=(near[face][1], rep),
            device_id_type=MESH,
        )

    def send_faces(field):
        for s in range(4):
            cube = T[field, s].reshape(8, 8, 8, 128)
            parts = (
                cube[0].reshape(64, 128), cube[7].reshape(64, 128),
                cube[:, 0].reshape(64, 128), cube[:, 7].reshape(64, 128),
                T[field, s, pl.ds(0, 64, stride=8), :], T[field, s, pl.ds(7, 64, stride=8), :],
            )
            for face, part in enumerate(parts):
                FB[field][OPP[face], s] = part.astype(BF16)
        for face in (4, 5, 2, 3, 0, 1):
            @pl.when(near[face][0])
            def _():
                face_copy(field, face).start()

    def wait_faces(field):
        for face in range(6):
            @pl.when(near[face][0])
            def _():
                arrival(field, face).wait_recv()

    def drain_faces(field):
        for face in range(6):
            @pl.when(near[face][0])
            def _():
                face_copy(field, face).wait_send()

    def halo(field, face, s):
        link = links[0, s, face]
        there = link >= 0
        safe = jnp.where(there, link, 0)
        index = safe % 4 + jnp.where(safe // 4 == space, 0, 4)
        index = jnp.where(there, index, 0)
        got = FB[field][face, index].astype(F32)
        return jnp.where(there, got, 0.0)

    level = lax.broadcasted_iota(jnp.int32, (1, 8, 128), 1)

    def down(cube):
        return pltpu.roll(cube, 1, 1)

    def up(cube):
        return pltpu.roll(cube, 7, 1)

    def put_centre(field, V):
        def body(i, carry):
            rows = [T[field, s, pl.ds(pl.multiple_of(i * 64, 64), 64), :].reshape(8, 8, 128) for s in range(4)]
            V[i + 1, 1:9, :, 128:256] = jnp.concatenate(rows, axis=1).astype(BF16)
            return carry

        lax.fori_loop(0, 8, body, 0)

    def put_halos(field, V):
        zero = jnp.zeros((32, 384), BF16)
        for i in (0, 9):
            for j in (0, 9):
                V[i, j] = zero
        for s in range(4):
            cube = T[field, s].reshape(64, 8, 128)
            U[0, s] = down(cube).reshape(512, 128)
            U[1, s] = up(cube).reshape(512, 128)
            U[0, s, pl.ds(0, 64, stride=8), :] = halo(field, 4, s)
            U[1, s, pl.ds(7, 64, stride=8), :] = halo(field, 5, s)

        def body(i, carry):
            for n, lane in ((0, 0), (1, 256)):
                rows = [U[n, s, pl.ds(pl.multiple_of(i * 64, 64), 64), :].reshape(8, 8, 128) for s in range(4)]
                V[i + 1, 1:9, :, lane:lane + 128] = jnp.concatenate(rows, axis=1).astype(BF16)
            return carry

        lax.fori_loop(0, 8, body, 0)
        for face in range(4):
            layers = [halo(field, face, s).reshape(8, 8, 128) for s in range(4)]
            lower = [jnp.where(level == 0, 0.0, down(layer)) for layer in layers]
            upper = [jnp.where(level == 7, 0.0, up(layer)) for layer in layers]
            for lane, group in ((0, lower), (128, layers), (256, upper)):
                value = jnp.concatenate(group, axis=1).astype(BF16)
                edge = 9 if face % 2 else 0
                if face < 2:
                    V[edge, 1:9, :, lane:lane + 128] = value
                else:
                    V[1:9, edge, :, lane:lane + 128] = value

    def convolve(V, W, emit, between=None):
        for half in range(2):
            if half and between is not None:
                between()
            groups = []
            for p in range(2):
                base = half * 4 + p * 2
                groups.append(jnp.concatenate(
                    [V[base + a, dj:dj + 8].reshape(256, 384) for a in range(4) for dj in range(3)], axis=1
                ))
            both = jnp.concatenate(groups, axis=0)
            total = jnp.dot(both, W[...], preferred_element_type=F32)
            for p in range(2):
                for h in range(2):
                    emit(half * 4 + p * 2 + h, total[p * 256:p * 256 + 256, h * 128:h * 128 + 128])

    def weight_product(G, V, which, between=None):
        columns = [(dj, dk) for dj in range(3) for dk in range(3)]
        for first in range(0, 9, 2):
            if first == 4 and between is not None:
                between()
            part = columns[first:first + 2]
            right = jnp.concatenate(
                [V[:, dj:dj + 8, :, dk * 128:dk * 128 + 128].reshape(2560, 128) for dj, dk in part], axis=1
            )
            R[which, :, first * 128:(first + len(part)) * 128] = jnp.dot(
                G[...], right, preferred_element_type=F32
            )

    def put_turned(G, i, rows):
        turned = rows.T.astype(BF16)
        for di in range(3):
            at = pl.multiple_of((i + di) * 256, 256)
            G[di * 128:di * 128 + 128, pl.ds(at, 256)] = turned

    def clear_turned(G):
        for di in range(3):
            for i in range(10):
                if not 0 <= i - di < 8:
                    G[di * 128:di * 128 + 128, i * 256:i * 256 + 256] = jnp.zeros((128, 256), BF16)

    def widen(W, source):
        blank = jnp.zeros((1152, 128), BF16)
        for a in range(4):
            W[a * 1152:a * 1152 + 1152, 0:128] = source[a] if a < 3 else blank
            W[a * 1152:a * 1152 + 1152, 128:256] = source[a - 1] if a > 0 else blank

    def widen_back(W, source):
        blank = jnp.zeros((1152, 128), BF16)
        W[3456:4608, 0:128] = blank
        W[0:1152, 128:256] = blank
        for a in range(3):
            for t in range(9):
                turned = source[2 - a, (8 - t) * 128:(8 - t) * 128 + 128, :].T
                W[a * 1152 + t * 128:a * 1152 + t * 128 + 128, 0:128] = turned
                W[(a + 1) * 1152 + t * 128:(a + 1) * 1152 + t * 128 + 128, 128:256] = turned

    def red_copy(which, slot, src, dst, peer):
        return pltpu.make_async_remote_copy(
            src_ref=src, dst_ref=dst, send_sem=red_send.at[which, slot],
            recv_sem=red_recv.at[which, slot], device_id=peer, device_id_type=MESH,
        )

    outs = (F0, F1)
    quarter = y * 2 + x
    my_row = pl.multiple_of(core * 192 + quarter * 48, 16)

    def quarter_of(d):
        return (1 - y if d & 2 else y) * 2 + (1 - x if d & 1 else x)

    def core_copy(w):
        other = pl.multiple_of((1 - core) * 192, 16)
        return red_copy(w, 0, R.at[w, pl.ds(other, 192)], A0.at[w], core_peer())

    def xy_copy(w, d):
        row = pl.multiple_of(quarter_of(d) * 48, 16)
        return red_copy(w, d, B0.at[w, pl.ds(row, 48)], XY.at[w, d - 1], xy_peer(d))

    def z_copy(w, d):
        lane = pl.multiple_of(z_far(d) * 256, 128)
        return red_copy(w, 3 + d, B1.at[w, :, pl.ds(lane, 384)], ZR.at[w, d - 1], z_peer(d))

    def z_back(w, d):
        ref = outs[w].at[pl.ds(my_row, 48), pl.ds(pl.multiple_of(z * 256, 128), 256)]
        return red_copy(w, 6 + d, ref, ref, z_peer(d))

    def z_from(w, d):
        ref = outs[w].at[pl.ds(my_row, 48), pl.ds(pl.multiple_of(z_far(d) * 256, 128), 256)]
        return red_copy(w, 6 + d, ref, ref, z_peer(d))

    def z_last(w, d):
        ref = outs[w].at[pl.ds(my_row, 48), pl.ds(1024, 128)]
        return red_copy(w, 9 + d, ref, ref, z_peer(d))

    def xy_back(w, d, mine):
        q = quarter if mine else quarter_of(d)
        ref = outs[w].at[pl.ds(pl.multiple_of(core * 192 + q * 48, 16), 48)]
        return red_copy(w, 12 + d, ref, ref, xy_peer(d))

    def core_back(w, mine):
        c = core if mine else 1 - core
        ref = outs[w].at[pl.ds(pl.multiple_of(c * 192, 16), 192)]
        return red_copy(w, 16, ref, ref, core_peer())

    D = (1, 2, 3)

    def red_start(w):
        core_copy(w).start()

    def red_xy(w):
        core_copy(w).wait()
        mine = pl.multiple_of(core * 192, 16)
        summed = R[w, pl.ds(mine, 192), :] + A0[w]
        R[w, pl.ds(mine, 192), :] = summed
        B0[w] = summed.astype(BF16)
        for d in (3, 1, 2):
            xy_copy(w, d).start()

    def red_z(w):
        for d in D:
            xy_copy(w, d).wait()
        summed = R[w, pl.ds(my_row, 48), :]
        for d in D:
            summed = summed + XY[w, d - 1].astype(F32)
        S1[w] = summed
        B1[w] = summed.astype(BF16)
        for d in (3, 2, 1):
            z_copy(w, d).start()

    def red_back_z(w):
        for d in D:
            z_copy(w, d).wait()
        summed = S1[w, :, pl.ds(pl.multiple_of(z * 256, 128), 384)]
        for d in D:
            summed = summed + ZR[w, d - 1].astype(F32)
        summed = summed.astype(BF16)
        outs[w][pl.ds(my_row, 48), pl.ds(pl.multiple_of(z * 256, 128), 256)] = summed[:, 0:256]
        for d in (3, 2, 1):
            z_back(w, d).start()

        @pl.when(z == 3)
        def _():
            outs[w][pl.ds(my_row, 48), pl.ds(1024, 128)] = summed[:, 256:384]
            for d in D:
                z_last(w, d).start()

    def red_back_xy(w):
        for d in D:
            z_from(w, d).wait_recv()
            @pl.when(z_far(d) == 3)
            def _():
                z_last(w, d).wait_recv()
        for d in (3, 1, 2):
            xy_back(w, d, True).start()

    def red_back_core(w):
        for d in D:
            xy_back(w, d, False).wait_recv()
        core_back(w, True).start()

    def red_end(w):
        core_back(w, False).wait_recv()
        core_back(w, True).wait_send()
        for d in D:
            xy_back(w, d, True).wait_send()
            z_back(w, d).wait_send()

        @pl.when(z == 3)
        def _():
            for d in D:
                z_last(w, d).wait_send()

    keep = [occ[0, s].astype(F32) for s in range(4)]
    slot_of = lax.broadcasted_iota(jnp.int32, (32, 128), 0) // 8
    mask = jnp.zeros((32, 128), F32)
    for s in range(4):
        mask = jnp.where(slot_of == s, keep[s], mask)
    mask = mask[None]

    def load(field, source):
        for s in range(4):
            T[field, s] = source[s].astype(F32) * keep[s]

    def masked_rows(rows):
        return (rows.reshape(8, 32, 128) * mask)

    def nothing():
        pass

    def when_here(*steps):
        def run():
            for step, which in steps:
                step(which)

        return run if reduce_here else nothing

    def finish(g, source):
        for di in range(3):
            for m in range(9):
                g[di * 9 + m] = source[di * 128:di * 128 + 128, m * 128:m * 128 + 128].T

    load(0, vox)
    send_faces(0)
    load(1, cot)
    send_faces(1)
    put_centre(0, VX)
    put_centre(1, VG)
    widen(WA, w1)
    clear_turned(GA)
    clear_turned(GB)

    def turn_out(i, carry):
        put_turned(GB, i, VG[i + 1, 1:9, :, 128:256].reshape(256, 128).astype(F32))
        return carry

    lax.fori_loop(0, 8, turn_out, 0)
    wait_faces(0)
    put_halos(0, VX)

    def emit_first(i, rows):
        FI[i] = rows
        hidden = masked_rows(rows * jax.nn.sigmoid(rows))
        for s in range(4):
            T[2, s, i * 64:i * 64 + 64, :] = hidden[:, s * 8:s * 8 + 8].reshape(64, 128)

    convolve(VX, WA, emit_first)
    send_faces(2)
    put_centre(2, VH)
    widen_back(WB, w2)
    widen(WC, w2)
    wait_faces(1)
    put_halos(1, VG)
    wait_faces(2)
    put_halos(2, VH)
    weight_product(GB, VH, 1)
    when_here((red_start, 1))()

    def emit_grad(i, rows):
        first = FI[i]
        sigma = jax.nn.sigmoid(first)
        grad = masked_rows(rows * sigma * (1.0 + first * (1.0 - sigma))).reshape(256, 128)
        put_turned(GA, i, grad)

    convolve(VG, WB, emit_grad, when_here((red_xy, 1)))
    weight_product(GA, VX, 0, when_here((red_z, 1)))
    when_here((red_start, 0))()

    def emit_out(i, rows):
        inner = VX[i + 1, 1:9, :, 128:256].astype(F32) + rows.reshape(8, 32, 128)
        inner = (inner * mask).astype(BF16).astype(F32)
        for s in range(4):
            out[s, i * 64:i * 64 + 64, :] = inner[:, s * 8:s * 8 + 8].reshape(64, 128).astype(BF16)

    convolve(VH, WC, emit_out, when_here((red_back_z, 1), (red_xy, 0)))
    if reduce_here:
        red_back_xy(1)
        red_z(0)
        red_back_core(1)
        red_back_z(0)
        red_end(1)
        red_back_xy(0)
        finish(g2, F1)
        red_back_core(0)
        red_end(0)
        finish(g1, F0)
    else:
        finish(g1, R.at[0])
        finish(g2, R.at[1])
    for field in range(3):
        drain_faces(field)


def solution(mesh):
    spaces, reps = mesh.shape["space"], mesh.shape["rep"]
    reduce_here = spaces == 8 and reps == 4
    grad_type = BF16 if reduce_here else F32

    def local(voxels, occupied, neighbours, first_weight, second_weight, cotangent):
        smem = pl.BlockSpec(memory_space=pltpu.SMEM)
        vmem = pl.BlockSpec(memory_space=pltpu.VMEM)
        out, first, second = pl.pallas_call(
            functools.partial(kernel, spaces, reps, reduce_here),
            out_shape=(
                jax.ShapeDtypeStruct((4, 512, 128), BF16),
                jax.ShapeDtypeStruct((27, 128, 128), grad_type),
                jax.ShapeDtypeStruct((27, 128, 128), grad_type),
            ),
            in_specs=[smem, smem, vmem, vmem, vmem, vmem],
            out_specs=(vmem, vmem, vmem),
            scratch_shapes=[
                pltpu.VMEM((3, 4, 512, 128), F32),
                pltpu.VMEM((2, 4, 512, 128), F32),
                pltpu.VMEM((6, 8, 64, 128), BF16),
                pltpu.VMEM((6, 8, 64, 128), BF16),
                pltpu.VMEM((6, 8, 64, 128), BF16),
                pltpu.VMEM((10, 10, 32, 384), BF16),
                pltpu.VMEM((10, 10, 32, 384), BF16),
                pltpu.VMEM((10, 10, 32, 384), BF16),
                pltpu.VMEM((4608, 256), BF16),
                pltpu.VMEM((4608, 256), BF16),
                pltpu.VMEM((4608, 256), BF16),
                pltpu.VMEM((8, 256, 128), F32),
                pltpu.VMEM((384, 2560), BF16),
                pltpu.VMEM((384, 2560), BF16),
                pltpu.VMEM((2, 384, 1152), F32),
                pltpu.VMEM((2, 192, 1152), F32),
                pltpu.VMEM((2, 192, 1152), BF16),
                pltpu.VMEM((2, 3, 48, 1152), BF16),
                pltpu.VMEM((2, 48, 1152), F32),
                pltpu.VMEM((2, 48, 1152), BF16),
                pltpu.VMEM((2, 3, 48, 384), BF16),
                pltpu.VMEM((384, 1152), BF16),
                pltpu.VMEM((384, 1152), BF16),
                pltpu.SemaphoreType.DMA((3, 6)),
                pltpu.SemaphoreType.DMA((3, 6)),
                pltpu.SemaphoreType.DMA((2, 17)),
                pltpu.SemaphoreType.DMA((2, 17)),
            ],
            compiler_params=pltpu.CompilerParams(
                collective_id=0, has_side_effects=True, vmem_limit_bytes=56 * 2**20
            ),
            cost_estimate=pl.CostEstimate(flops=9_060_000_000, bytes_accessed=6_000_000, transcendentals=500_000),
        )(
            occupied, neighbours, voxels.reshape(4, 512, 128),
            first_weight.reshape(3, 1152, 128), second_weight.reshape(3, 1152, 128),
            cotangent.reshape(4, 512, 128),
        )
        if not reduce_here:
            first, second = lax.psum((first, second), ("space", "rep"))

        return out[None], first.astype(F32), second.astype(F32)

    placed = (
        P("rep", "space", None, None),
        P("rep", "space"),
        P("rep", "space", None),
        P(),
        P(),
        P("rep", "space", None, None),
    )
    return jax.shard_map(
        local,
        mesh=mesh,
        in_specs=placed,
        out_specs=(P("rep", "space", None, None), P(), P()),
        check_vma=False,
    )
```

```python
import functools

import jax
import jax.numpy as jnp
from jax import lax
from jax.experimental import pallas as pl
from jax.experimental.pallas import tpu as pltpu
from jax.sharding import PartitionSpec as P

MESH = pl.DeviceIdType.MESH
OPP = (1, 0, 3, 2, 5, 4)
F32 = jnp.float32
BF16 = jnp.bfloat16


def spread(number, start):
    return [(2 * place + start, place) for place in range(number)]


def eye(size):
    row = lax.broadcasted_iota(jnp.int32, (size, size), 0)
    column = lax.broadcasted_iota(jnp.int32, (size, size), 1)
    return (row == column).astype(F32).astype(BF16)


def last_by_last(left, right):
    return lax.dot_general(left, right, (((1,), (1,)), ((), ())), preferred_element_type=F32)


def turn_kernel(first, second, g1, g2):
    for source, g in ((first, g1), (second, g2)):
        for m in range(0, 9, 2):
            count = min(2, 9 - m)
            block = source[:, m * 128:(m + count) * 128]
            turned = last_by_last(eye(count * 128), block)
            for n in range(count):
                g[m + n] = turned[n * 128:n * 128 + 128]


def tile_place(device, spaces):
    plane = spaces.bit_length() - 2
    wide, tall = (plane + 1) // 2, plane // 2
    column = sum(device // 2**src % 2 * 2**dst for src, dst in spread(wide, 0))
    row = sum(device // 2**src % 2 * 2**dst for src, dst in spread(tall, 1))
    layer = device // 2**plane
    return column, row, layer


def tile_owner(column, row, layer, spaces):
    plane = spaces.bit_length() - 2
    wide, tall = (plane + 1) // 2, plane // 2
    owner = layer * 2**plane
    owner = owner + sum(column // 2**dst % 2 * 2**src for src, dst in spread(wide, 0))
    return owner + sum(row // 2**dst % 2 * 2**src for src, dst in spread(tall, 1))


def tile_neighbours(device, spaces):
    plane = spaces.bit_length() - 2
    sizes = (2 ** ((plane + 1) // 2), 2 ** (plane // 2), 2)
    place = tile_place(device, spaces)
    found = []
    for face in range(6):
        dim, step = face // 2, 1 if face % 2 else -1
        moved = list(place)
        moved[dim] = (moved[dim] + step + sizes[dim]) % sizes[dim]
        there = place[dim] < sizes[dim] - 1 if face % 2 else place[dim] > 0
        found.append((there, tile_owner(*moved, spaces)))
    return found


def kernel(
    spaces, reps, reduce_here,
    occ, links, vox, w1, w2, cot,
    out, F0, F1,
    T, U, FB0, FB1, FB2, VX, VH, VG, WA, WB, WC, FI, GA, GB, R, A0, B0, XA, ZA, SA, BA, XB, ZB, SB, BB,
    face_send, face_recv, red_send, red_recv,
):
    FB = (FB0, FB1, FB2)
    space, rep = lax.axis_index("space"), lax.axis_index("rep")
    near = tile_neighbours(space, spaces)
    x, z, y, core = space % 2, space // 2, rep // 2, rep % 2

    def core_peer():
        return (space, y * 2 + (1 - core))

    def xy_peer(d):
        flipped_x = 1 - x if d & 1 else x
        flipped_y = 1 - y if d & 2 else y
        return (z * 2 + flipped_x, flipped_y * 2 + core)

    def z_far(d):
        low = 1 - z % 2 if d & 1 else z % 2
        high = 1 - z // 2 if d & 2 else z // 2
        return high * 2 + low

    def z_peer(d):
        return (z_far(d) * 2 + x, rep)

    barrier = pltpu.get_barrier_semaphore()
    if reduce_here:
        peers = [core_peer()] + [xy_peer(d) for d in (1, 2, 3)] + [z_peer(d) for d in (1, 2, 3)]
        for peer in peers:
            pl.semaphore_signal(barrier, inc=1, device_id=peer, device_id_type=MESH)
        pl.semaphore_wait(barrier, 7)
    else:
        total = 0
        for there, owner in near:
            total = total + there.astype(jnp.int32)

            @pl.when(there)
            def _():
                pl.semaphore_signal(barrier, inc=1, device_id=(owner, rep), device_id_type=MESH)

        pl.semaphore_wait(barrier, total)

    def face_copy(field, face):
        return pltpu.make_async_remote_copy(
            src_ref=FB[field].at[OPP[face], pl.ds(0, 4)],
            dst_ref=FB[field].at[OPP[face], pl.ds(4, 4)],
            send_sem=face_send.at[field, face],
            recv_sem=face_recv.at[field, OPP[face]],
            device_id=(near[face][1], rep),
            device_id_type=MESH,
        )

    def arrival(field, face):
        return pltpu.make_async_remote_copy(
            src_ref=FB[field].at[face, pl.ds(0, 4)],
            dst_ref=FB[field].at[face, pl.ds(4, 4)],
            send_sem=face_send.at[field, face],
            recv_sem=face_recv.at[field, face],
            device_id=(near[face][1], rep),
            device_id_type=MESH,
        )

    def send_faces(field):
        for s in range(4):
            cube = T[field, s].reshape(8, 8, 8, 128)
            parts = (
                cube[0].reshape(64, 128), cube[7].reshape(64, 128),
                cube[:, 0].reshape(64, 128), cube[:, 7].reshape(64, 128),
                T[field, s, pl.ds(0, 64, stride=8), :], T[field, s, pl.ds(7, 64, stride=8), :],
            )
            for face, part in enumerate(parts):
                FB[field][OPP[face], s] = part.astype(BF16)
        for face in (4, 5, 2, 3, 0, 1):
            @pl.when(near[face][0])
            def _():
                face_copy(field, face).start()

    def wait_faces(field):
        for face in range(6):
            @pl.when(near[face][0])
            def _():
                arrival(field, face).wait_recv()

    def drain_faces(field):
        for face in range(6):
            @pl.when(near[face][0])
            def _():
                face_copy(field, face).wait_send()

    def halo(field, face, s):
        link = links[0, s, face]
        there = link >= 0
        safe = jnp.where(there, link, 0)
        index = safe % 4 + jnp.where(safe // 4 == space, 0, 4)
        index = jnp.where(there, index, 0)
        got = FB[field][face, index].astype(F32)
        return jnp.where(there, got, 0.0)

    level = lax.broadcasted_iota(jnp.int32, (1, 8, 128), 1)

    def down(cube):
        return pltpu.roll(cube, 1, 1)

    def up(cube):
        return pltpu.roll(cube, 7, 1)

    def put_centre(field, V):
        def body(i, carry):
            rows = [T[field, s, pl.ds(pl.multiple_of(i * 64, 64), 64), :].reshape(8, 8, 128) for s in range(4)]
            V[i + 1, 1:9, :, 128:256] = jnp.concatenate(rows, axis=1).astype(BF16)
            return carry

        lax.fori_loop(0, 8, body, 0)

    def put_halos(field, V):
        zero = jnp.zeros((32, 384), BF16)
        for i in (0, 9):
            for j in (0, 9):
                V[i, j] = zero
        for s in range(4):
            cube = T[field, s].reshape(64, 8, 128)
            U[0, s] = down(cube).reshape(512, 128)
            U[1, s] = up(cube).reshape(512, 128)
            U[0, s, pl.ds(0, 64, stride=8), :] = halo(field, 4, s)
            U[1, s, pl.ds(7, 64, stride=8), :] = halo(field, 5, s)

        def body(i, carry):
            for n, lane in ((0, 0), (1, 256)):
                rows = [U[n, s, pl.ds(pl.multiple_of(i * 64, 64), 64), :].reshape(8, 8, 128) for s in range(4)]
                V[i + 1, 1:9, :, lane:lane + 128] = jnp.concatenate(rows, axis=1).astype(BF16)
            return carry

        lax.fori_loop(0, 8, body, 0)
        for face in range(4):
            layers = [halo(field, face, s).reshape(8, 8, 128) for s in range(4)]
            lower = [jnp.where(level == 0, 0.0, down(layer)) for layer in layers]
            upper = [jnp.where(level == 7, 0.0, up(layer)) for layer in layers]
            for lane, group in ((0, lower), (128, layers), (256, upper)):
                value = jnp.concatenate(group, axis=1).astype(BF16)
                edge = 9 if face % 2 else 0
                if face < 2:
                    V[edge, 1:9, :, lane:lane + 128] = value
                else:
                    V[1:9, edge, :, lane:lane + 128] = value

    def convolve(V, W, emit, between=None, back=False):
        for half in range(2):
            if half and between is not None:
                between()
            groups = []
            for p in range(2):
                base = half * 4 + p * 2
                groups.append(jnp.concatenate(
                    [V[base + a, dj:dj + 8].reshape(256, 384) for a in range(4) for dj in range(3)], axis=1
                ))
            both = jnp.concatenate(groups, axis=0)
            if back:
                total = last_by_last(both, W[...])
            else:
                total = jnp.dot(both, W[...], preferred_element_type=F32)
            for p in range(2):
                for h in range(2):
                    emit(half * 4 + p * 2 + h, total[p * 256:p * 256 + 256, h * 128:h * 128 + 128])

    def weight_product(G, V, which, between=None):
        columns = [(dj, dk) for dj in range(3) for dk in range(3)]
        for first in range(0, 9, 2):
            if first == 4 and between is not None:
                between()
            part = columns[first:first + 2]
            right = jnp.concatenate(
                [V[:, dj:dj + 8, :, dk * 128:dk * 128 + 128].reshape(2560, 128) for dj, dk in part], axis=1
            )
            R[which, :, first * 128:(first + len(part)) * 128] = jnp.dot(
                G[...], right, preferred_element_type=F32
            )

    unit = eye(128)

    def put_turned(G, i, rows):
        turned = last_by_last(unit, rows).astype(BF16)
        for di in range(3):
            at = pl.multiple_of((i + di) * 256, 256)
            G[di * 128:di * 128 + 128, pl.ds(at, 256)] = turned

    def clear_turned(G):
        for di in range(3):
            for i in range(10):
                if not 0 <= i - di < 8:
                    G[di * 128:di * 128 + 128, i * 256:i * 256 + 256] = jnp.zeros((128, 256), BF16)

    def widen(W, source):
        blank = jnp.zeros((1152, 128), BF16)
        for a in range(4):
            W[a * 1152:a * 1152 + 1152, 0:128] = source[a] if a < 3 else blank
            W[a * 1152:a * 1152 + 1152, 128:256] = source[a - 1] if a > 0 else blank

    def widen_back(W, source):
        blank = jnp.zeros((128, 1152), BF16)
        W[0:128, 3456:4608] = blank
        W[128:256, 0:1152] = blank
        for a in range(3):
            for t in range(9):
                piece = source[2 - a, (8 - t) * 128:(8 - t) * 128 + 128, :]
                lane = a * 1152 + t * 128
                W[0:128, lane:lane + 128] = piece
                W[128:256, lane + 1152:lane + 1280] = piece

    def red_copy(which, slot, src, dst, peer):
        return pltpu.make_async_remote_copy(
            src_ref=src, dst_ref=dst, send_sem=red_send.at[which, slot],
            recv_sem=red_recv.at[which, slot], device_id=peer, device_id_type=MESH,
        )

    outs = (F0, F1)
    quarter = y * 2 + x
    D = (1, 2, 3)
    top = pl.multiple_of(core * 192, 16)
    low = pl.multiple_of(core * 192 + 128, 16)
    row_a = pl.multiple_of(core * 192 + quarter * 32, 16)
    row_b = pl.multiple_of(core * 192 + 128 + quarter * 16, 16)

    def quarter_of(d):
        return (1 - y if d & 2 else y) * 2 + (1 - x if d & 1 else x)

    def lanes(place, width):
        return pl.ds(pl.multiple_of(place * 256, 128), width)

    def core_copy(w):
        other = pl.multiple_of((1 - core) * 192, 16)
        return red_copy(w, 0, R.at[w, pl.ds(other, 192)], A0.at[w], core_peer())

    def a_xy(w, d):
        row = pl.multiple_of(quarter_of(d) * 32, 16)
        return red_copy(w, d, B0.at[w, pl.ds(row, 32)], XA.at[w, d - 1], xy_peer(d))

    def a_z(w, d):
        return red_copy(w, 3 + d, BA.at[w, :, lanes(z_far(d), 384)], ZA.at[w, d - 1], z_peer(d))

    def a_back_z(w, d, place):
        ref = outs[w].at[pl.ds(row_a, 32), lanes(place, 256)]
        return red_copy(w, 6 + d, ref, ref, z_peer(d))

    def a_last_z(w, d):
        ref = outs[w].at[pl.ds(row_a, 32), pl.ds(1024, 128)]
        return red_copy(w, 9 + d, ref, ref, z_peer(d))

    def a_back_xy(w, d, q):
        ref = outs[w].at[pl.ds(pl.multiple_of(core * 192 + q * 32, 16), 32)]
        return red_copy(w, 12 + d, ref, ref, xy_peer(d))

    def b_z(w, d):
        return red_copy(w, 15 + d, B0.at[w, pl.ds(128, 64), lanes(z_far(d), 384)], ZB.at[w, d - 1], z_peer(d))

    def b_xy(w, d):
        row = pl.multiple_of(quarter_of(d) * 16, 16)
        return red_copy(w, 18 + d, BB.at[w, pl.ds(row, 16)], XB.at[w, d - 1], xy_peer(d))

    def b_rows(q):
        return pl.ds(pl.multiple_of(core * 192 + 128 + q * 16, 16), 16)

    def b_back_xy(w, d, q):
        ref = outs[w].at[b_rows(q), lanes(z, 256)]
        return red_copy(w, 21 + d, ref, ref, xy_peer(d))

    def b_last_xy(w, d, q):
        ref = outs[w].at[b_rows(q), pl.ds(1024, 128)]
        return red_copy(w, 24 + d, ref, ref, xy_peer(d))

    def b_back_z(w, d, place):
        ref = outs[w].at[pl.ds(low, 64), lanes(place, 256)]
        return red_copy(w, 27 + d, ref, ref, z_peer(d))

    def b_last_z(w, d):
        ref = outs[w].at[pl.ds(low, 64), pl.ds(1024, 128)]
        return red_copy(w, 30 + d, ref, ref, z_peer(d))

    def core_back(w, c):
        ref = outs[w].at[pl.ds(pl.multiple_of(c * 192, 16), 192)]
        return red_copy(w, 34, ref, ref, core_peer())

    def red_start(w):
        core_copy(w).start()

    def red_first(w):
        core_copy(w).wait()
        summed = R[w, pl.ds(top, 192), :] + A0[w]
        R[w, pl.ds(top, 192), :] = summed
        B0[w] = summed.astype(BF16)
        for d in (3, 1, 2):
            a_xy(w, d).start()
            b_z(w, d).start()

    def red_second(w):
        for d in D:
            a_xy(w, d).wait()
        summed = R[w, pl.ds(row_a, 32), :]
        for d in D:
            summed = summed + XA[w, d - 1].astype(F32)
        SA[w] = summed
        BA[w] = summed.astype(BF16)
        for d in (3, 2, 1):
            a_z(w, d).start()
        for d in D:
            b_z(w, d).wait()
        summed = R[w, pl.ds(low, 64), lanes(z, 384)]
        for d in D:
            summed = summed + ZB[w, d - 1].astype(F32)
        SB[w] = summed
        BB[w] = summed.astype(BF16)
        for d in (3, 1, 2):
            b_xy(w, d).start()

    def red_third(w):
        for d in D:
            a_z(w, d).wait()
        summed = SA[w, :, lanes(z, 384)]
        for d in D:
            summed = summed + ZA[w, d - 1].astype(F32)
        whole_a = summed.astype(BF16)
        outs[w][pl.ds(row_a, 32), lanes(z, 256)] = whole_a[:, 0:256]
        for d in (3, 2, 1):
            a_back_z(w, d, z).start()
        for d in D:
            b_xy(w, d).wait()
        summed = SB[w, pl.ds(pl.multiple_of(quarter * 16, 16), 16), :]
        for d in D:
            summed = summed + XB[w, d - 1].astype(F32)
        whole_b = summed.astype(BF16)
        outs[w][pl.ds(row_b, 16), lanes(z, 256)] = whole_b[:, 0:256]
        for d in (3, 1, 2):
            b_back_xy(w, d, quarter).start()

        @pl.when(z == 3)
        def _():
            outs[w][pl.ds(row_a, 32), pl.ds(1024, 128)] = whole_a[:, 256:384]
            outs[w][pl.ds(row_b, 16), pl.ds(1024, 128)] = whole_b[:, 256:384]
            for d in D:
                a_last_z(w, d).start()
                b_last_xy(w, d, quarter).start()

    def red_fourth(w):
        for d in D:
            a_back_z(w, d, z_far(d)).wait_recv()

            @pl.when(z_far(d) == 3)
            def _():
                a_last_z(w, d).wait_recv()
        for d in (3, 1, 2):
            a_back_xy(w, d, quarter).start()
        for d in D:
            b_back_xy(w, d, quarter_of(d)).wait_recv()
        for d in (3, 2, 1):
            b_back_z(w, d, z).start()

        @pl.when(z == 3)
        def _():
            for d in D:
                b_last_xy(w, d, quarter_of(d)).wait_recv()
            for d in D:
                b_last_z(w, d).start()

    def red_fifth(w):
        for d in D:
            a_back_xy(w, d, quarter_of(d)).wait_recv()
            b_back_z(w, d, z_far(d)).wait_recv()

            @pl.when(z_far(d) == 3)
            def _():
                b_last_z(w, d).wait_recv()
        core_back(w, core).start()

    def red_end(w):
        core_back(w, 1 - core).wait_recv()
        core_back(w, core).wait_send()
        for d in D:
            a_back_z(w, d, z).wait_send()
            a_back_xy(w, d, quarter).wait_send()
            b_back_xy(w, d, quarter).wait_send()
            b_back_z(w, d, z).wait_send()

        @pl.when(z == 3)
        def _():
            for d in D:
                a_last_z(w, d).wait_send()
                b_last_xy(w, d, quarter).wait_send()
                b_last_z(w, d).wait_send()

    keep = [occ[0, s].astype(F32) for s in range(4)]
    slot_of = lax.broadcasted_iota(jnp.int32, (32, 128), 0) // 8
    mask = jnp.zeros((32, 128), F32)
    for s in range(4):
        mask = jnp.where(slot_of == s, keep[s], mask)
    mask = mask[None]

    def load(field, source):
        for s in range(4):
            T[field, s] = source[s].astype(F32) * keep[s]

    def masked_rows(rows):
        return (rows.reshape(8, 32, 128) * mask)

    def nothing():
        pass

    def when_here(*steps):
        def run():
            for step, which in steps:
                step(which)

        return run if reduce_here else nothing

    load(0, vox)
    send_faces(0)
    load(1, cot)
    send_faces(1)
    put_centre(0, VX)
    put_centre(1, VG)
    widen(WA, w1)
    clear_turned(GA)
    clear_turned(GB)

    def turn_out(i, carry):
        put_turned(GB, i, VG[i + 1, 1:9, :, 128:256].reshape(256, 128))
        return carry

    lax.fori_loop(0, 8, turn_out, 0)
    wait_faces(0)
    put_halos(0, VX)

    def emit_first(i, rows):
        FI[i] = rows
        hidden = masked_rows(rows * jax.nn.sigmoid(rows))
        for s in range(4):
            T[2, s, i * 64:i * 64 + 64, :] = hidden[:, s * 8:s * 8 + 8].reshape(64, 128)

    convolve(VX, WA, emit_first)
    send_faces(2)
    put_centre(2, VH)
    widen_back(WB, w2)
    widen(WC, w2)
    wait_faces(1)
    put_halos(1, VG)
    wait_faces(2)
    put_halos(2, VH)
    weight_product(GB, VH, 1)
    when_here((red_start, 1))()

    def emit_grad(i, rows):
        first = FI[i]
        sigma = jax.nn.sigmoid(first)
        grad = masked_rows(rows * sigma * (1.0 + first * (1.0 - sigma))).reshape(256, 128)
        put_turned(GA, i, grad.astype(BF16))

    convolve(VG, WB, emit_grad, when_here((red_first, 1)), True)
    weight_product(GA, VX, 0, when_here((red_second, 1)))
    when_here((red_start, 0))()

    def emit_out(i, rows):
        inner = VX[i + 1, 1:9, :, 128:256].astype(F32) + rows.reshape(8, 32, 128)
        inner = (inner * mask).astype(BF16).astype(F32)
        for s in range(4):
            out[s, i * 64:i * 64 + 64, :] = inner[:, s * 8:s * 8 + 8].reshape(64, 128).astype(BF16)

    convolve(VH, WC, emit_out, when_here((red_third, 1), (red_first, 0)))
    if reduce_here:
        red_fourth(1)
        red_second(0)
        red_fifth(1)
        red_third(0)
        red_end(1)
        red_fourth(0)
        red_fifth(0)
        red_end(0)
    else:
        F0[...] = R[0]
        F1[...] = R[1]
    for field in range(3):
        drain_faces(field)


def solution(mesh):
    spaces, reps = mesh.shape["space"], mesh.shape["rep"]
    reduce_here = spaces == 8 and reps == 4
    grad_type = BF16 if reduce_here else F32

    def local(voxels, occupied, neighbours, first_weight, second_weight, cotangent):
        smem = pl.BlockSpec(memory_space=pltpu.SMEM)
        vmem = pl.BlockSpec(memory_space=pltpu.VMEM)
        out, first, second = pl.pallas_call(
            functools.partial(kernel, spaces, reps, reduce_here),
            out_shape=(
                jax.ShapeDtypeStruct((4, 512, 128), BF16),
                jax.ShapeDtypeStruct((384, 1152), grad_type),
                jax.ShapeDtypeStruct((384, 1152), grad_type),
            ),
            in_specs=[smem, smem, vmem, vmem, vmem, vmem],
            out_specs=(vmem, vmem, vmem),
            scratch_shapes=[
                pltpu.VMEM((3, 4, 512, 128), F32),
                pltpu.VMEM((2, 4, 512, 128), F32),
                pltpu.VMEM((6, 8, 64, 128), BF16),
                pltpu.VMEM((6, 8, 64, 128), BF16),
                pltpu.VMEM((6, 8, 64, 128), BF16),
                pltpu.VMEM((10, 10, 32, 384), BF16),
                pltpu.VMEM((10, 10, 32, 384), BF16),
                pltpu.VMEM((10, 10, 32, 384), BF16),
                pltpu.VMEM((4608, 256), BF16),
                pltpu.VMEM((256, 4608), BF16),
                pltpu.VMEM((4608, 256), BF16),
                pltpu.VMEM((8, 256, 128), F32),
                pltpu.VMEM((384, 2560), BF16),
                pltpu.VMEM((384, 2560), BF16),
                pltpu.VMEM((2, 384, 1152), F32),
                pltpu.VMEM((2, 192, 1152), F32),
                pltpu.VMEM((2, 192, 1152), BF16),
                pltpu.VMEM((2, 3, 32, 1152), BF16),
                pltpu.VMEM((2, 3, 32, 384), BF16),
                pltpu.VMEM((2, 32, 1152), F32),
                pltpu.VMEM((2, 32, 1152), BF16),
                pltpu.VMEM((2, 3, 16, 384), BF16),
                pltpu.VMEM((2, 3, 64, 384), BF16),
                pltpu.VMEM((2, 64, 384), F32),
                pltpu.VMEM((2, 64, 384), BF16),
                pltpu.SemaphoreType.DMA((3, 6)),
                pltpu.SemaphoreType.DMA((3, 6)),
                pltpu.SemaphoreType.DMA((2, 35)),
                pltpu.SemaphoreType.DMA((2, 35)),
            ],
            compiler_params=pltpu.CompilerParams(
                collective_id=0, has_side_effects=True, vmem_limit_bytes=56 * 2**20
            ),
            cost_estimate=pl.CostEstimate(flops=9_060_000_000, bytes_accessed=6_000_000, transcendentals=500_000),
        )(
            occupied, neighbours, voxels.reshape(4, 512, 128),
            first_weight.reshape(3, 1152, 128), second_weight.reshape(3, 1152, 128),
            cotangent.reshape(4, 512, 128),
        )
        if reduce_here:
            first, second = pl.pallas_call(
                turn_kernel,
                grid=(3,),
                out_shape=[jax.ShapeDtypeStruct((27, 128, 128), F32)] * 2,
                in_specs=[pl.BlockSpec((128, 1152), lambda i: (i, 0))] * 2,
                out_specs=[pl.BlockSpec((9, 128, 128), lambda i: (i, 0, 0))] * 2,
            )(first, second)
            return out[None], first, second
        first, second = lax.psum((first, second), ("space", "rep"))

        def turned(grad):
            return grad.reshape(3, 128, 9, 128).transpose(0, 2, 3, 1).reshape(27, 128, 128)

        return out[None], turned(first), turned(second)

    placed = (
        P("rep", "space", None, None),
        P("rep", "space"),
        P("rep", "space", None),
        P(),
        P(),
        P("rep", "space", None, None),
    )
    return jax.shard_map(
        local,
        mesh=mesh,
        in_specs=placed,
        out_specs=(P("rep", "space", None, None), P(), P()),
        check_vma=False,
    )
```

```python
import functools

import jax
import jax.numpy as jnp
from jax import lax
from jax.experimental import pallas as pl
from jax.experimental.pallas import tpu as pltpu
from jax.sharding import PartitionSpec as P

MESH = pl.DeviceIdType.MESH
OPP = (1, 0, 3, 2, 5, 4)
F32 = jnp.float32
BF16 = jnp.bfloat16


def spread(number, start):
    return [(2 * place + start, place) for place in range(number)]


def eye(size):
    row = lax.broadcasted_iota(jnp.int32, (size, size), 0)
    column = lax.broadcasted_iota(jnp.int32, (size, size), 1)
    return (row == column).astype(F32).astype(BF16)


def last_by_last(left, right):
    return lax.dot_general(left, right, (((1,), (1,)), ((), ())), preferred_element_type=F32)


def turn_kernel(first, second, g1, g2):
    unit = eye(384)
    for source, g in ((first, g1), (second, g2)):
        g[...] = last_by_last(unit, source[...]).reshape(3, 128, 128)


def tile_place(device, spaces):
    plane = spaces.bit_length() - 2
    wide, tall = (plane + 1) // 2, plane // 2
    column = sum(device // 2**src % 2 * 2**dst for src, dst in spread(wide, 0))
    row = sum(device // 2**src % 2 * 2**dst for src, dst in spread(tall, 1))
    layer = device // 2**plane
    return column, row, layer


def tile_owner(column, row, layer, spaces):
    plane = spaces.bit_length() - 2
    wide, tall = (plane + 1) // 2, plane // 2
    owner = layer * 2**plane
    owner = owner + sum(column // 2**dst % 2 * 2**src for src, dst in spread(wide, 0))
    return owner + sum(row // 2**dst % 2 * 2**src for src, dst in spread(tall, 1))


def tile_neighbours(device, spaces):
    plane = spaces.bit_length() - 2
    sizes = (2 ** ((plane + 1) // 2), 2 ** (plane // 2), 2)
    place = tile_place(device, spaces)
    found = []
    for face in range(6):
        dim, step = face // 2, 1 if face % 2 else -1
        moved = list(place)
        moved[dim] = (moved[dim] + step + sizes[dim]) % sizes[dim]
        there = place[dim] < sizes[dim] - 1 if face % 2 else place[dim] > 0
        found.append((there, tile_owner(*moved, spaces)))
    return found


def kernel(
    spaces, reps, reduce_here,
    occ, links, vox, w1, w2, cot,
    out, F0, F1,
    T, U, FB0, FB1, FB2, VX, VH, VG, WA, WB, WC, FI, GA, GB, R, A0, B0, XA, ZA, SA, BA, XB, ZB, SB, BB,
    face_send, face_recv, red_send, red_recv,
):
    FB = (FB0, FB1, FB2)
    space, rep = lax.axis_index("space"), lax.axis_index("rep")
    near = tile_neighbours(space, spaces)
    x, z, y, core = space % 2, space // 2, rep // 2, rep % 2

    def core_peer():
        return (space, y * 2 + (1 - core))

    def xy_peer(d):
        flipped_x = 1 - x if d & 1 else x
        flipped_y = 1 - y if d & 2 else y
        return (z * 2 + flipped_x, flipped_y * 2 + core)

    def z_far(d):
        low = 1 - z % 2 if d & 1 else z % 2
        high = 1 - z // 2 if d & 2 else z // 2
        return high * 2 + low

    def z_peer(d):
        return (z_far(d) * 2 + x, rep)

    barrier = pltpu.get_barrier_semaphore()
    if reduce_here:
        peers = [core_peer()] + [xy_peer(d) for d in (1, 2, 3)] + [z_peer(d) for d in (1, 2, 3)]
        for peer in peers:
            pl.semaphore_signal(barrier, inc=1, device_id=peer, device_id_type=MESH)
        pl.semaphore_wait(barrier, 7)
    else:
        total = 0
        for there, owner in near:
            total = total + there.astype(jnp.int32)

            @pl.when(there)
            def _():
                pl.semaphore_signal(barrier, inc=1, device_id=(owner, rep), device_id_type=MESH)

        pl.semaphore_wait(barrier, total)

    def face_copy(field, face):
        return pltpu.make_async_remote_copy(
            src_ref=FB[field].at[OPP[face], pl.ds(0, 4)],
            dst_ref=FB[field].at[OPP[face], pl.ds(4, 4)],
            send_sem=face_send.at[field, face],
            recv_sem=face_recv.at[field, OPP[face]],
            device_id=(near[face][1], rep),
            device_id_type=MESH,
        )

    def arrival(field, face):
        return pltpu.make_async_remote_copy(
            src_ref=FB[field].at[face, pl.ds(0, 4)],
            dst_ref=FB[field].at[face, pl.ds(4, 4)],
            send_sem=face_send.at[field, face],
            recv_sem=face_recv.at[field, face],
            device_id=(near[face][1], rep),
            device_id_type=MESH,
        )

    def send_faces(field):
        for s in range(4):
            cube = T[field, s].reshape(8, 8, 8, 128)
            parts = (
                cube[0].reshape(64, 128), cube[7].reshape(64, 128),
                cube[:, 0].reshape(64, 128), cube[:, 7].reshape(64, 128),
                T[field, s, pl.ds(0, 64, stride=8), :], T[field, s, pl.ds(7, 64, stride=8), :],
            )
            for face, part in enumerate(parts):
                FB[field][OPP[face], s] = part.astype(BF16)
        for face in (4, 5, 2, 3, 0, 1):
            @pl.when(near[face][0])
            def _():
                face_copy(field, face).start()

    def wait_faces(field):
        for face in range(6):
            @pl.when(near[face][0])
            def _():
                arrival(field, face).wait_recv()

    def drain_faces(field):
        for face in range(6):
            @pl.when(near[face][0])
            def _():
                face_copy(field, face).wait_send()

    def halo(field, face, s):
        link = links[0, s, face]
        there = link >= 0
        safe = jnp.where(there, link, 0)
        index = safe % 4 + jnp.where(safe // 4 == space, 0, 4)
        index = jnp.where(there, index, 0)
        got = FB[field][face, index].astype(F32)
        return jnp.where(there, got, 0.0)

    level = lax.broadcasted_iota(jnp.int32, (1, 8, 128), 1)

    def down(cube):
        return pltpu.roll(cube, 1, 1)

    def up(cube):
        return pltpu.roll(cube, 7, 1)

    def put_centre(field, V):
        def body(i, carry):
            rows = [T[field, s, pl.ds(pl.multiple_of(i * 64, 64), 64), :].reshape(8, 8, 128) for s in range(4)]
            V[i + 1, 1:9, :, 128:256] = jnp.concatenate(rows, axis=1).astype(BF16)
            return carry

        lax.fori_loop(0, 8, body, 0)

    def put_halos(field, V):
        zero = jnp.zeros((32, 384), BF16)
        for i in (0, 9):
            for j in (0, 9):
                V[i, j] = zero
        for s in range(4):
            cube = T[field, s].reshape(64, 8, 128)
            U[0, s] = down(cube).reshape(512, 128)
            U[1, s] = up(cube).reshape(512, 128)
            U[0, s, pl.ds(0, 64, stride=8), :] = halo(field, 4, s)
            U[1, s, pl.ds(7, 64, stride=8), :] = halo(field, 5, s)

        def body(i, carry):
            for n, lane in ((0, 0), (1, 256)):
                rows = [U[n, s, pl.ds(pl.multiple_of(i * 64, 64), 64), :].reshape(8, 8, 128) for s in range(4)]
                V[i + 1, 1:9, :, lane:lane + 128] = jnp.concatenate(rows, axis=1).astype(BF16)
            return carry

        lax.fori_loop(0, 8, body, 0)
        for face in range(4):
            layers = [halo(field, face, s).reshape(8, 8, 128) for s in range(4)]
            lower = [jnp.where(level == 0, 0.0, down(layer)) for layer in layers]
            upper = [jnp.where(level == 7, 0.0, up(layer)) for layer in layers]
            for lane, group in ((0, lower), (128, layers), (256, upper)):
                value = jnp.concatenate(group, axis=1).astype(BF16)
                edge = 9 if face % 2 else 0
                if face < 2:
                    V[edge, 1:9, :, lane:lane + 128] = value
                else:
                    V[1:9, edge, :, lane:lane + 128] = value

    def convolve(V, W, emit, between=None, back=False):
        for half in range(2):
            if half and between is not None:
                between()
            groups = []
            for p in range(2):
                base = half * 4 + p * 2
                groups.append(jnp.concatenate(
                    [V[base + a, dj:dj + 8].reshape(256, 384) for a in range(4) for dj in range(3)], axis=1
                ))
            both = jnp.concatenate(groups, axis=0)
            if back:
                total = last_by_last(both, W[...])
            else:
                total = jnp.dot(both, W[...], preferred_element_type=F32)
            for p in range(2):
                for h in range(2):
                    emit(half * 4 + p * 2 + h, total[p * 256:p * 256 + 256, h * 128:h * 128 + 128])

    def weight_product(G, V, which, start, count):
        columns = [(dj, dk) for dj in range(3) for dk in range(3)]
        for first in range(0, 9, 2):
            part = columns[first:first + 2]
            right = jnp.concatenate(
                [V[:, dj:dj + 8, :, dk * 128:dk * 128 + 128].reshape(2560, 128) for dj, dk in part], axis=1
            )
            R[which, pl.ds(start, count), first * 128:(first + len(part)) * 128] = jnp.dot(
                G[pl.ds(start, count), :], right, preferred_element_type=F32
            )

    unit = eye(128)

    def put_turned(G, i, rows):
        turned = last_by_last(unit, rows).astype(BF16)
        for di in range(3):
            at = pl.multiple_of((i + di) * 256, 256)
            G[di * 128:di * 128 + 128, pl.ds(at, 256)] = turned

    def clear_turned(G):
        for di in range(3):
            for i in range(10):
                if not 0 <= i - di < 8:
                    G[di * 128:di * 128 + 128, i * 256:i * 256 + 256] = jnp.zeros((128, 256), BF16)

    def widen(W, source):
        blank = jnp.zeros((1152, 128), BF16)
        for a in range(4):
            W[a * 1152:a * 1152 + 1152, 0:128] = source[a] if a < 3 else blank
            W[a * 1152:a * 1152 + 1152, 128:256] = source[a - 1] if a > 0 else blank

    def widen_back(W, source):
        blank = jnp.zeros((128, 1152), BF16)
        W[0:128, 3456:4608] = blank
        W[128:256, 0:1152] = blank
        for a in range(3):
            for t in range(9):
                piece = source[2 - a, (8 - t) * 128:(8 - t) * 128 + 128, :]
                lane = a * 1152 + t * 128
                W[0:128, lane:lane + 128] = piece
                W[128:256, lane + 1152:lane + 1280] = piece

    def red_copy(which, slot, src, dst, peer):
        return pltpu.make_async_remote_copy(
            src_ref=src, dst_ref=dst, send_sem=red_send.at[which, slot],
            recv_sem=red_recv.at[which, slot], device_id=peer, device_id_type=MESH,
        )

    outs = (F0, F1)
    quarter = y * 2 + x
    D = (1, 2, 3)
    top = pl.multiple_of(core * 192, 16)
    low = pl.multiple_of(core * 192 + 128, 16)
    row_a = pl.multiple_of(core * 192 + quarter * 32, 16)
    row_b = pl.multiple_of(core * 192 + 128 + quarter * 16, 16)

    def quarter_of(d):
        return (1 - y if d & 2 else y) * 2 + (1 - x if d & 1 else x)

    def lanes(place, width):
        return pl.ds(pl.multiple_of(place * 256, 128), width)

    def core_copy(w):
        other = pl.multiple_of((1 - core) * 192, 16)
        return red_copy(w, 0, R.at[w, pl.ds(other, 192)], A0.at[w], core_peer())

    def a_xy(w, d):
        row = pl.multiple_of(quarter_of(d) * 32, 16)
        return red_copy(w, d, B0.at[w, pl.ds(row, 32)], XA.at[w, d - 1], xy_peer(d))

    def a_z(w, d):
        return red_copy(w, 3 + d, BA.at[w, :, lanes(z_far(d), 384)], ZA.at[w, d - 1], z_peer(d))

    def a_back_z(w, d, place):
        ref = outs[w].at[pl.ds(row_a, 32), lanes(place, 256)]
        return red_copy(w, 6 + d, ref, ref, z_peer(d))

    def a_last_z(w, d):
        ref = outs[w].at[pl.ds(row_a, 32), pl.ds(1024, 128)]
        return red_copy(w, 9 + d, ref, ref, z_peer(d))

    def a_back_xy(w, d, q):
        ref = outs[w].at[pl.ds(pl.multiple_of(core * 192 + q * 32, 16), 32)]
        return red_copy(w, 12 + d, ref, ref, xy_peer(d))

    def b_z(w, d):
        return red_copy(w, 15 + d, B0.at[w, pl.ds(128, 64), lanes(z_far(d), 384)], ZB.at[w, d - 1], z_peer(d))

    def b_xy(w, d):
        row = pl.multiple_of(quarter_of(d) * 16, 16)
        return red_copy(w, 18 + d, BB.at[w, pl.ds(row, 16)], XB.at[w, d - 1], xy_peer(d))

    def b_rows(q):
        return pl.ds(pl.multiple_of(core * 192 + 128 + q * 16, 16), 16)

    def b_back_xy(w, d, q):
        ref = outs[w].at[b_rows(q), lanes(z, 256)]
        return red_copy(w, 21 + d, ref, ref, xy_peer(d))

    def b_last_xy(w, d, q):
        ref = outs[w].at[b_rows(q), pl.ds(1024, 128)]
        return red_copy(w, 24 + d, ref, ref, xy_peer(d))

    def b_back_z(w, d, place):
        ref = outs[w].at[pl.ds(low, 64), lanes(place, 256)]
        return red_copy(w, 27 + d, ref, ref, z_peer(d))

    def b_last_z(w, d):
        ref = outs[w].at[pl.ds(low, 64), pl.ds(1024, 128)]
        return red_copy(w, 30 + d, ref, ref, z_peer(d))

    def core_back(w, c):
        ref = outs[w].at[pl.ds(pl.multiple_of(c * 192, 16), 192)]
        return red_copy(w, 34, ref, ref, core_peer())

    def red_start(w):
        core_copy(w).start()

    def red_first(w):
        core_copy(w).wait()
        summed = R[w, pl.ds(top, 192), :] + A0[w]
        R[w, pl.ds(top, 192), :] = summed
        B0[w] = summed.astype(BF16)
        for d in (3, 1, 2):
            a_xy(w, d).start()
            b_z(w, d).start()

    def red_second(w):
        for d in D:
            a_xy(w, d).wait()
        summed = R[w, pl.ds(row_a, 32), :]
        for d in D:
            summed = summed + XA[w, d - 1].astype(F32)
        SA[w] = summed
        BA[w] = summed.astype(BF16)
        for d in (3, 2, 1):
            a_z(w, d).start()
        for d in D:
            b_z(w, d).wait()
        summed = R[w, pl.ds(low, 64), lanes(z, 384)]
        for d in D:
            summed = summed + ZB[w, d - 1].astype(F32)
        SB[w] = summed
        BB[w] = summed.astype(BF16)
        for d in (3, 1, 2):
            b_xy(w, d).start()

    def red_third(w):
        for d in D:
            a_z(w, d).wait()
        summed = SA[w, :, lanes(z, 384)]
        for d in D:
            summed = summed + ZA[w, d - 1].astype(F32)
        whole_a = summed.astype(BF16)
        outs[w][pl.ds(row_a, 32), lanes(z, 256)] = whole_a[:, 0:256]
        for d in (3, 2, 1):
            a_back_z(w, d, z).start()
        for d in D:
            b_xy(w, d).wait()
        summed = SB[w, pl.ds(pl.multiple_of(quarter * 16, 16), 16), :]
        for d in D:
            summed = summed + XB[w, d - 1].astype(F32)
        whole_b = summed.astype(BF16)
        outs[w][pl.ds(row_b, 16), lanes(z, 256)] = whole_b[:, 0:256]
        for d in (3, 1, 2):
            b_back_xy(w, d, quarter).start()

        @pl.when(z == 3)
        def _():
            outs[w][pl.ds(row_a, 32), pl.ds(1024, 128)] = whole_a[:, 256:384]
            outs[w][pl.ds(row_b, 16), pl.ds(1024, 128)] = whole_b[:, 256:384]
            for d in D:
                a_last_z(w, d).start()
                b_last_xy(w, d, quarter).start()

    def red_fourth(w):
        for d in D:
            a_back_z(w, d, z_far(d)).wait_recv()

            @pl.when(z_far(d) == 3)
            def _():
                a_last_z(w, d).wait_recv()
        for d in (3, 1, 2):
            a_back_xy(w, d, quarter).start()
        for d in D:
            b_back_xy(w, d, quarter_of(d)).wait_recv()
        for d in (3, 2, 1):
            b_back_z(w, d, z).start()

        @pl.when(z == 3)
        def _():
            for d in D:
                b_last_xy(w, d, quarter_of(d)).wait_recv()
            for d in D:
                b_last_z(w, d).start()

    def red_fifth(w):
        for d in D:
            a_back_xy(w, d, quarter_of(d)).wait_recv()
            b_back_z(w, d, z_far(d)).wait_recv()

            @pl.when(z_far(d) == 3)
            def _():
                b_last_z(w, d).wait_recv()
        core_back(w, core).start()

    def red_end(w):
        core_back(w, 1 - core).wait_recv()
        core_back(w, core).wait_send()
        for d in D:
            a_back_z(w, d, z).wait_send()
            a_back_xy(w, d, quarter).wait_send()
            b_back_xy(w, d, quarter).wait_send()
            b_back_z(w, d, z).wait_send()

        @pl.when(z == 3)
        def _():
            for d in D:
                a_last_z(w, d).wait_send()
                b_last_xy(w, d, quarter).wait_send()
                b_last_z(w, d).wait_send()

    keep = [occ[0, s].astype(F32) for s in range(4)]
    slot_of = lax.broadcasted_iota(jnp.int32, (32, 128), 0) // 8
    mask = jnp.zeros((32, 128), F32)
    for s in range(4):
        mask = jnp.where(slot_of == s, keep[s], mask)
    mask = mask[None]

    def load(field, source):
        for s in range(4):
            T[field, s] = source[s].astype(F32) * keep[s]

    def masked_rows(rows):
        return (rows.reshape(8, 32, 128) * mask)

    load(0, vox)
    send_faces(0)
    load(1, cot)
    send_faces(1)
    put_centre(0, VX)
    put_centre(1, VG)
    widen(WA, w1)
    clear_turned(GA)
    clear_turned(GB)

    def turn_out(i, carry):
        put_turned(GB, i, VG[i + 1, 1:9, :, 128:256].reshape(256, 128))
        return carry

    lax.fori_loop(0, 8, turn_out, 0)
    wait_faces(0)
    put_halos(0, VX)

    def emit_first(i, rows):
        FI[i] = rows
        hidden = masked_rows(rows * jax.nn.sigmoid(rows))
        for s in range(4):
            T[2, s, i * 64:i * 64 + 64, :] = hidden[:, s * 8:s * 8 + 8].reshape(64, 128)

    convolve(VX, WA, emit_first)
    send_faces(2)
    put_centre(2, VH)
    widen_back(WB, w2)
    widen(WC, w2)
    wait_faces(1)
    put_halos(1, VG)

    def emit_grad(i, rows):
        first = FI[i]
        sigma = jax.nn.sigmoid(first)
        grad = masked_rows(rows * sigma * (1.0 + first * (1.0 - sigma))).reshape(256, 128)
        put_turned(GA, i, grad.astype(BF16))

    def emit_out(i, rows):
        inner = VX[i + 1, 1:9, :, 128:256].astype(F32) + rows.reshape(8, 32, 128)
        inner = (inner * mask).astype(BF16).astype(F32)
        for s in range(4):
            out[s, i * 64:i * 64 + 64, :] = inner[:, s * 8:s * 8 + 8].reshape(64, 128).astype(BF16)

    convolve(VG, WB, emit_grad, None, True)
    if reduce_here:
        away = pl.multiple_of((1 - core) * 192, 16)
        weight_product(GA, VX, 0, away, 192)
        red_start(0)
        weight_product(GA, VX, 0, top, 192)
        red_first(0)
        wait_faces(2)
        put_halos(2, VH)
        weight_product(GB, VH, 1, away, 192)
        red_start(1)
        red_second(0)
        weight_product(GB, VH, 1, top, 192)
        red_first(1)
        red_third(0)

        def between():
            red_second(1)
            red_fourth(0)

        convolve(VH, WC, emit_out, between)
        red_third(1)
        red_fifth(0)
        red_fourth(1)
        red_end(0)
        red_fifth(1)
        red_end(1)
    else:
        weight_product(GA, VX, 0, 0, 384)
        wait_faces(2)
        put_halos(2, VH)
        weight_product(GB, VH, 1, 0, 384)
        convolve(VH, WC, emit_out)
        F0[...] = R[0]
        F1[...] = R[1]
    for field in range(3):
        drain_faces(field)


def solution(mesh):
    spaces, reps = mesh.shape["space"], mesh.shape["rep"]
    reduce_here = spaces == 8 and reps == 4
    grad_type = BF16 if reduce_here else F32

    def local(voxels, occupied, neighbours, first_weight, second_weight, cotangent):
        smem = pl.BlockSpec(memory_space=pltpu.SMEM)
        vmem = pl.BlockSpec(memory_space=pltpu.VMEM)
        out, first, second = pl.pallas_call(
            functools.partial(kernel, spaces, reps, reduce_here),
            out_shape=(
                jax.ShapeDtypeStruct((4, 512, 128), BF16),
                jax.ShapeDtypeStruct((384, 1152), grad_type),
                jax.ShapeDtypeStruct((384, 1152), grad_type),
            ),
            in_specs=[smem, smem, vmem, vmem, vmem, vmem],
            out_specs=(vmem, vmem, vmem),
            scratch_shapes=[
                pltpu.VMEM((3, 4, 512, 128), F32),
                pltpu.VMEM((2, 4, 512, 128), F32),
                pltpu.VMEM((6, 8, 64, 128), BF16),
                pltpu.VMEM((6, 8, 64, 128), BF16),
                pltpu.VMEM((6, 8, 64, 128), BF16),
                pltpu.VMEM((10, 10, 32, 384), BF16),
                pltpu.VMEM((10, 10, 32, 384), BF16),
                pltpu.VMEM((10, 10, 32, 384), BF16),
                pltpu.VMEM((4608, 256), BF16),
                pltpu.VMEM((256, 4608), BF16),
                pltpu.VMEM((4608, 256), BF16),
                pltpu.VMEM((8, 256, 128), F32),
                pltpu.VMEM((384, 2560), BF16),
                pltpu.VMEM((384, 2560), BF16),
                pltpu.VMEM((2, 384, 1152), F32),
                pltpu.VMEM((2, 192, 1152), F32),
                pltpu.VMEM((2, 192, 1152), BF16),
                pltpu.VMEM((2, 3, 32, 1152), BF16),
                pltpu.VMEM((2, 3, 32, 384), BF16),
                pltpu.VMEM((2, 32, 1152), F32),
                pltpu.VMEM((2, 32, 1152), BF16),
                pltpu.VMEM((2, 3, 16, 384), BF16),
                pltpu.VMEM((2, 3, 64, 384), BF16),
                pltpu.VMEM((2, 64, 384), F32),
                pltpu.VMEM((2, 64, 384), BF16),
                pltpu.SemaphoreType.DMA((3, 6)),
                pltpu.SemaphoreType.DMA((3, 6)),
                pltpu.SemaphoreType.DMA((2, 35)),
                pltpu.SemaphoreType.DMA((2, 35)),
            ],
            compiler_params=pltpu.CompilerParams(
                collective_id=0, has_side_effects=True, vmem_limit_bytes=56 * 2**20
            ),
            cost_estimate=pl.CostEstimate(flops=9_060_000_000, bytes_accessed=6_000_000, transcendentals=500_000),
        )(
            occupied, neighbours, voxels.reshape(4, 512, 128),
            first_weight.reshape(3, 1152, 128), second_weight.reshape(3, 1152, 128),
            cotangent.reshape(4, 512, 128),
        )
        if reduce_here:
            first, second = pl.pallas_call(
                turn_kernel,
                grid=(3, 3),
                out_shape=[jax.ShapeDtypeStruct((27, 128, 128), F32)] * 2,
                in_specs=[pl.BlockSpec((128, 384), lambda i, j: (i, j))] * 2,
                out_specs=[pl.BlockSpec((3, 128, 128), lambda i, j: (i * 3 + j, 0, 0))] * 2,
            )(first, second)
            return out[None], first, second
        first, second = lax.psum((first, second), ("space", "rep"))

        def turned(grad):
            return grad.reshape(3, 128, 9, 128).transpose(0, 2, 3, 1).reshape(27, 128, 128)

        return out[None], turned(first), turned(second)

    placed = (
        P("rep", "space", None, None),
        P("rep", "space"),
        P("rep", "space", None),
        P(),
        P(),
        P("rep", "space", None, None),
    )
    return jax.shard_map(
        local,
        mesh=mesh,
        in_specs=placed,
        out_specs=(P("rep", "space", None, None), P(), P()),
        check_vma=False,
    )
```

```python
import functools

import jax
import jax.numpy as jnp
from jax import lax
from jax.experimental import pallas as pl
from jax.experimental.pallas import tpu as pltpu
from jax.sharding import PartitionSpec as P

MESH = pl.DeviceIdType.MESH
OPP = (1, 0, 3, 2, 5, 4)
F32 = jnp.float32
BF16 = jnp.bfloat16


def spread(number, start):
    return [(2 * place + start, place) for place in range(number)]


def eye(size):
    row = lax.broadcasted_iota(jnp.int32, (size, size), 0)
    column = lax.broadcasted_iota(jnp.int32, (size, size), 1)
    return (row == column).astype(F32).astype(BF16)


def last_by_last(left, right):
    return lax.dot_general(left, right, (((1,), (1,)), ((), ())), preferred_element_type=F32)


def turn(source, g, base):
    for m in range(0, 9, 2):
        count = min(2, 9 - m)
        turned = last_by_last(eye(count * 128), source[:, m * 128:(m + count) * 128])
        for n in range(count):
            g[base + m + n] = turned[n * 128:n * 128 + 128].astype(g.dtype)


def turn_kernel(first, second, g1, g2):
    g1[...] = first[...].astype(F32)
    turn(second, g2, 0)


def tile_place(device, spaces):
    plane = spaces.bit_length() - 2
    wide, tall = (plane + 1) // 2, plane // 2
    column = sum(device // 2**src % 2 * 2**dst for src, dst in spread(wide, 0))
    row = sum(device // 2**src % 2 * 2**dst for src, dst in spread(tall, 1))
    layer = device // 2**plane
    return column, row, layer


def tile_owner(column, row, layer, spaces):
    plane = spaces.bit_length() - 2
    wide, tall = (plane + 1) // 2, plane // 2
    owner = layer * 2**plane
    owner = owner + sum(column // 2**dst % 2 * 2**src for src, dst in spread(wide, 0))
    return owner + sum(row // 2**dst % 2 * 2**src for src, dst in spread(tall, 1))


def tile_neighbours(device, spaces):
    plane = spaces.bit_length() - 2
    sizes = (2 ** ((plane + 1) // 2), 2 ** (plane // 2), 2)
    place = tile_place(device, spaces)
    found = []
    for face in range(6):
        dim, step = face // 2, 1 if face % 2 else -1
        moved = list(place)
        moved[dim] = (moved[dim] + step + sizes[dim]) % sizes[dim]
        there = place[dim] < sizes[dim] - 1 if face % 2 else place[dim] > 0
        found.append((there, tile_owner(*moved, spaces)))
    return found


def kernel(
    spaces, reps, reduce_here,
    occ, links, vox, w1, w2, cot,
    out, g1, F1,
    T, U, FB0, FB1, FB2, VX, VH, VG, WA, WB, WC, FI, GA, GB, R, A0, B0, XA, ZA, SA, BA, XB, ZB, SB, BB, F0,
    face_send, face_recv, red_send, red_recv,
):
    FB = (FB0, FB1, FB2)
    space, rep = lax.axis_index("space"), lax.axis_index("rep")
    near = tile_neighbours(space, spaces)
    x, z, y, core = space % 2, space // 2, rep // 2, rep % 2

    def core_peer():
        return (space, y * 2 + (1 - core))

    def xy_peer(d):
        flipped_x = 1 - x if d & 1 else x
        flipped_y = 1 - y if d & 2 else y
        return (z * 2 + flipped_x, flipped_y * 2 + core)

    def z_far(d):
        low = 1 - z % 2 if d & 1 else z % 2
        high = 1 - z // 2 if d & 2 else z // 2
        return high * 2 + low

    def z_peer(d):
        return (z_far(d) * 2 + x, rep)

    barrier = pltpu.get_barrier_semaphore()
    if reduce_here:
        peers = [core_peer()] + [xy_peer(d) for d in (1, 2, 3)] + [z_peer(d) for d in (1, 2, 3)]
        for peer in peers:
            pl.semaphore_signal(barrier, inc=1, device_id=peer, device_id_type=MESH)
        pl.semaphore_wait(barrier, 7)
    else:
        total = 0
        for there, owner in near:
            total = total + there.astype(jnp.int32)

            @pl.when(there)
            def _():
                pl.semaphore_signal(barrier, inc=1, device_id=(owner, rep), device_id_type=MESH)

        pl.semaphore_wait(barrier, total)

    def face_copy(field, face):
        return pltpu.make_async_remote_copy(
            src_ref=FB[field].at[OPP[face], pl.ds(0, 4)],
            dst_ref=FB[field].at[OPP[face], pl.ds(4, 4)],
            send_sem=face_send.at[field, face],
            recv_sem=face_recv.at[field, OPP[face]],
            device_id=(near[face][1], rep),
            device_id_type=MESH,
        )

    def arrival(field, face):
        return pltpu.make_async_remote_copy(
            src_ref=FB[field].at[face, pl.ds(0, 4)],
            dst_ref=FB[field].at[face, pl.ds(4, 4)],
            send_sem=face_send.at[field, face],
            recv_sem=face_recv.at[field, face],
            device_id=(near[face][1], rep),
            device_id_type=MESH,
        )

    def send_faces(field):
        for s in range(4):
            cube = T[field, s].reshape(8, 8, 8, 128)
            parts = (
                cube[0].reshape(64, 128), cube[7].reshape(64, 128),
                cube[:, 0].reshape(64, 128), cube[:, 7].reshape(64, 128),
                T[field, s, pl.ds(0, 64, stride=8), :], T[field, s, pl.ds(7, 64, stride=8), :],
            )
            for face, part in enumerate(parts):
                FB[field][OPP[face], s] = part.astype(BF16)
        for face in (4, 5, 2, 3, 0, 1):
            @pl.when(near[face][0])
            def _():
                face_copy(field, face).start()

    def wait_faces(field):
        for face in range(6):
            @pl.when(near[face][0])
            def _():
                arrival(field, face).wait_recv()

    def drain_faces(field):
        for face in range(6):
            @pl.when(near[face][0])
            def _():
                face_copy(field, face).wait_send()

    def halo(field, face, s):
        link = links[0, s, face]
        there = link >= 0
        safe = jnp.where(there, link, 0)
        index = safe % 4 + jnp.where(safe // 4 == space, 0, 4)
        index = jnp.where(there, index, 0)
        got = FB[field][face, index].astype(F32)
        return jnp.where(there, got, 0.0)

    level = lax.broadcasted_iota(jnp.int32, (1, 8, 128), 1)

    def down(cube):
        return pltpu.roll(cube, 1, 1)

    def up(cube):
        return pltpu.roll(cube, 7, 1)

    def put_centre(field, V):
        def body(i, carry):
            rows = [T[field, s, pl.ds(pl.multiple_of(i * 64, 64), 64), :].reshape(8, 8, 128) for s in range(4)]
            V[i + 1, 1:9, :, 128:256] = jnp.concatenate(rows, axis=1).astype(BF16)
            return carry

        lax.fori_loop(0, 8, body, 0)

    def put_halos(field, V):
        zero = jnp.zeros((32, 384), BF16)
        for i in (0, 9):
            for j in (0, 9):
                V[i, j] = zero
        for s in range(4):
            cube = T[field, s].reshape(64, 8, 128)
            U[0, s] = down(cube).reshape(512, 128)
            U[1, s] = up(cube).reshape(512, 128)
            U[0, s, pl.ds(0, 64, stride=8), :] = halo(field, 4, s)
            U[1, s, pl.ds(7, 64, stride=8), :] = halo(field, 5, s)

        def body(i, carry):
            for n, lane in ((0, 0), (1, 256)):
                rows = [U[n, s, pl.ds(pl.multiple_of(i * 64, 64), 64), :].reshape(8, 8, 128) for s in range(4)]
                V[i + 1, 1:9, :, lane:lane + 128] = jnp.concatenate(rows, axis=1).astype(BF16)
            return carry

        lax.fori_loop(0, 8, body, 0)
        for face in range(4):
            layers = [halo(field, face, s).reshape(8, 8, 128) for s in range(4)]
            lower = [jnp.where(level == 0, 0.0, down(layer)) for layer in layers]
            upper = [jnp.where(level == 7, 0.0, up(layer)) for layer in layers]
            for lane, group in ((0, lower), (128, layers), (256, upper)):
                value = jnp.concatenate(group, axis=1).astype(BF16)
                edge = 9 if face % 2 else 0
                if face < 2:
                    V[edge, 1:9, :, lane:lane + 128] = value
                else:
                    V[1:9, edge, :, lane:lane + 128] = value

    def convolve(V, W, emit, between=None):
        for half in range(2):
            if half and between is not None:
                between()
            groups = []
            for p in range(2):
                base = half * 4 + p * 2
                groups.append(jnp.concatenate(
                    [V[base + a, dj:dj + 8].reshape(256, 384) for a in range(4) for dj in range(3)], axis=1
                ))
            both = jnp.concatenate(groups, axis=0)
            total = jnp.dot(both, W[...], preferred_element_type=F32)
            for p in range(2):
                for h in range(2):
                    emit(half * 4 + p * 2 + h, total[p * 256:p * 256 + 256, h * 128:h * 128 + 128])

    def weight_product(G, V, which, start, count):
        columns = [(dj, dk) for dj in range(3) for dk in range(3)]
        for first in range(0, 9, 2):
            part = columns[first:first + 2]
            right = jnp.concatenate(
                [V[:, dj:dj + 8, :, dk * 128:dk * 128 + 128].reshape(2560, 128) for dj, dk in part], axis=1
            )
            R[which, pl.ds(start, count), first * 128:(first + len(part)) * 128] = jnp.dot(
                G[pl.ds(start, count), :], right, preferred_element_type=F32
            )

    unit = eye(128)

    def put_turned(G, i, rows):
        turned = last_by_last(unit, rows).astype(BF16)
        for di in range(3):
            at = pl.multiple_of((i + di) * 256, 256)
            G[di * 128:di * 128 + 128, pl.ds(at, 256)] = turned

    def clear_turned(G):
        for di in range(3):
            for i in range(10):
                if not 0 <= i - di < 8:
                    G[di * 128:di * 128 + 128, i * 256:i * 256 + 256] = jnp.zeros((128, 256), BF16)

    def widen(W, source):
        blank = jnp.zeros((1152, 128), BF16)
        for a in range(4):
            W[a * 1152:a * 1152 + 1152, 0:128] = source[a] if a < 3 else blank
            W[a * 1152:a * 1152 + 1152, 128:256] = source[a - 1] if a > 0 else blank

    def widen_back(W, source):
        blank = jnp.zeros((1152, 128), BF16)
        W[3456:4608, 0:128] = blank
        W[0:1152, 128:256] = blank
        for a in range(3):
            for t in range(9):
                turned = source[2 - a, (8 - t) * 128:(8 - t) * 128 + 128, :].T
                row = a * 1152 + t * 128
                W[row:row + 128, 0:128] = turned
                W[row + 1152:row + 1280, 128:256] = turned

    def red_copy(which, slot, src, dst, peer):
        return pltpu.make_async_remote_copy(
            src_ref=src, dst_ref=dst, send_sem=red_send.at[which, slot],
            recv_sem=red_recv.at[which, slot], device_id=peer, device_id_type=MESH,
        )

    outs = (F0, F1)
    quarter = y * 2 + x
    D = (1, 2, 3)
    top = pl.multiple_of(core * 192, 16)
    low = pl.multiple_of(core * 192 + 128, 16)
    row_a = pl.multiple_of(core * 192 + quarter * 32, 16)
    row_b = pl.multiple_of(core * 192 + 128 + quarter * 16, 16)

    def quarter_of(d):
        return (1 - y if d & 2 else y) * 2 + (1 - x if d & 1 else x)

    def lanes(place, width):
        return pl.ds(pl.multiple_of(place * 256, 128), width)

    def core_copy(w):
        other = pl.multiple_of((1 - core) * 192, 16)
        return red_copy(w, 0, R.at[w, pl.ds(other, 192)], A0.at[w], core_peer())

    def a_xy(w, d):
        row = pl.multiple_of(quarter_of(d) * 32, 16)
        return red_copy(w, d, B0.at[w, pl.ds(row, 32)], XA.at[w, d - 1], xy_peer(d))

    def a_z(w, d):
        return red_copy(w, 3 + d, BA.at[w, :, lanes(z_far(d), 384)], ZA.at[w, d - 1], z_peer(d))

    def a_back_z(w, d, place):
        ref = outs[w].at[pl.ds(row_a, 32), lanes(place, 256)]
        return red_copy(w, 6 + d, ref, ref, z_peer(d))

    def a_last_z(w, d):
        ref = outs[w].at[pl.ds(row_a, 32), pl.ds(1024, 128)]
        return red_copy(w, 9 + d, ref, ref, z_peer(d))

    def a_back_xy(w, d, q):
        ref = outs[w].at[pl.ds(pl.multiple_of(core * 192 + q * 32, 16), 32)]
        return red_copy(w, 12 + d, ref, ref, xy_peer(d))

    def b_z(w, d):
        return red_copy(w, 15 + d, B0.at[w, pl.ds(128, 64), lanes(z_far(d), 384)], ZB.at[w, d - 1], z_peer(d))

    def b_xy(w, d):
        row = pl.multiple_of(quarter_of(d) * 16, 16)
        return red_copy(w, 18 + d, BB.at[w, pl.ds(row, 16)], XB.at[w, d - 1], xy_peer(d))

    def b_rows(q):
        return pl.ds(pl.multiple_of(core * 192 + 128 + q * 16, 16), 16)

    def b_back_xy(w, d, q):
        ref = outs[w].at[b_rows(q), lanes(z, 256)]
        return red_copy(w, 21 + d, ref, ref, xy_peer(d))

    def b_last_xy(w, d, q):
        ref = outs[w].at[b_rows(q), pl.ds(1024, 128)]
        return red_copy(w, 24 + d, ref, ref, xy_peer(d))

    def b_back_z(w, d, place):
        ref = outs[w].at[pl.ds(low, 64), lanes(place, 256)]
        return red_copy(w, 27 + d, ref, ref, z_peer(d))

    def b_last_z(w, d):
        ref = outs[w].at[pl.ds(low, 64), pl.ds(1024, 128)]
        return red_copy(w, 30 + d, ref, ref, z_peer(d))

    def core_back(w, c):
        ref = outs[w].at[pl.ds(pl.multiple_of(c * 192, 16), 192)]
        return red_copy(w, 34, ref, ref, core_peer())

    def red_start(w):
        core_copy(w).start()

    def red_first(w):
        core_copy(w).wait()
        summed = R[w, pl.ds(top, 192), :] + A0[w]
        R[w, pl.ds(top, 192), :] = summed
        B0[w] = summed.astype(BF16)
        for d in (3, 1, 2):
            a_xy(w, d).start()
            b_z(w, d).start()

    def red_second(w):
        for d in D:
            a_xy(w, d).wait()
        summed = R[w, pl.ds(row_a, 32), :]
        for d in D:
            summed = summed + XA[w, d - 1].astype(F32)
        SA[w] = summed
        BA[w] = summed.astype(BF16)
        for d in (3, 2, 1):
            a_z(w, d).start()
        for d in D:
            b_z(w, d).wait()
        summed = R[w, pl.ds(low, 64), lanes(z, 384)]
        for d in D:
            summed = summed + ZB[w, d - 1].astype(F32)
        SB[w] = summed
        BB[w] = summed.astype(BF16)
        for d in (3, 1, 2):
            b_xy(w, d).start()

    def red_third(w):
        for d in D:
            a_z(w, d).wait()
        summed = SA[w, :, lanes(z, 384)]
        for d in D:
            summed = summed + ZA[w, d - 1].astype(F32)
        whole_a = summed.astype(BF16)
        outs[w][pl.ds(row_a, 32), lanes(z, 256)] = whole_a[:, 0:256]
        for d in (3, 2, 1):
            a_back_z(w, d, z).start()
        for d in D:
            b_xy(w, d).wait()
        summed = SB[w, pl.ds(pl.multiple_of(quarter * 16, 16), 16), :]
        for d in D:
            summed = summed + XB[w, d - 1].astype(F32)
        whole_b = summed.astype(BF16)
        outs[w][pl.ds(row_b, 16), lanes(z, 256)] = whole_b[:, 0:256]
        for d in (3, 1, 2):
            b_back_xy(w, d, quarter).start()

        @pl.when(z == 3)
        def _():
            outs[w][pl.ds(row_a, 32), pl.ds(1024, 128)] = whole_a[:, 256:384]
            outs[w][pl.ds(row_b, 16), pl.ds(1024, 128)] = whole_b[:, 256:384]
            for d in D:
                a_last_z(w, d).start()
                b_last_xy(w, d, quarter).start()

    def red_fourth(w):
        for d in D:
            a_back_z(w, d, z_far(d)).wait_recv()

            @pl.when(z_far(d) == 3)
            def _():
                a_last_z(w, d).wait_recv()
        for d in (3, 1, 2):
            a_back_xy(w, d, quarter).start()
        for d in D:
            b_back_xy(w, d, quarter_of(d)).wait_recv()
        for d in (3, 2, 1):
            b_back_z(w, d, z).start()

        @pl.when(z == 3)
        def _():
            for d in D:
                b_last_xy(w, d, quarter_of(d)).wait_recv()
            for d in D:
                b_last_z(w, d).start()

    def red_fifth(w):
        for d in D:
            a_back_xy(w, d, quarter_of(d)).wait_recv()
            b_back_z(w, d, z_far(d)).wait_recv()

            @pl.when(z_far(d) == 3)
            def _():
                b_last_z(w, d).wait_recv()
        core_back(w, core).start()

    def red_end(w):
        core_back(w, 1 - core).wait_recv()
        core_back(w, core).wait_send()
        for d in D:
            a_back_z(w, d, z).wait_send()
            a_back_xy(w, d, quarter).wait_send()
            b_back_xy(w, d, quarter).wait_send()
            b_back_z(w, d, z).wait_send()

        @pl.when(z == 3)
        def _():
            for d in D:
                a_last_z(w, d).wait_send()
                b_last_xy(w, d, quarter).wait_send()
                b_last_z(w, d).wait_send()

    keep = [occ[0, s].astype(F32) for s in range(4)]
    slot_of = lax.broadcasted_iota(jnp.int32, (32, 128), 0) // 8
    mask = jnp.zeros((32, 128), F32)
    for s in range(4):
        mask = jnp.where(slot_of == s, keep[s], mask)
    mask = mask[None]

    def load(field, source):
        for s in range(4):
            T[field, s] = source[s].astype(F32) * keep[s]

    def masked_rows(rows):
        return (rows.reshape(8, 32, 128) * mask)

    load(0, vox)
    send_faces(0)
    load(1, cot)
    send_faces(1)
    put_centre(0, VX)
    put_centre(1, VG)
    widen(WA, w1)
    clear_turned(GA)
    clear_turned(GB)

    def turn_out(i, carry):
        put_turned(GB, i, VG[i + 1, 1:9, :, 128:256].reshape(256, 128))
        return carry

    lax.fori_loop(0, 8, turn_out, 0)
    wait_faces(0)
    put_halos(0, VX)

    def emit_first(i, rows):
        FI[i] = rows
        hidden = masked_rows(rows * jax.nn.sigmoid(rows))
        for s in range(4):
            T[2, s, i * 64:i * 64 + 64, :] = hidden[:, s * 8:s * 8 + 8].reshape(64, 128)

    convolve(VX, WA, emit_first)
    send_faces(2)
    put_centre(2, VH)
    widen_back(WB, w2)
    widen(WC, w2)
    wait_faces(1)
    put_halos(1, VG)

    def emit_grad(i, rows):
        first = FI[i]
        sigma = jax.nn.sigmoid(first)
        grad = masked_rows(rows * sigma * (1.0 + first * (1.0 - sigma))).reshape(256, 128)
        put_turned(GA, i, grad.astype(BF16))

    def emit_out(i, rows):
        inner = VX[i + 1, 1:9, :, 128:256].astype(F32) + rows.reshape(8, 32, 128)
        inner = (inner * mask).astype(BF16).astype(F32)
        for s in range(4):
            out[s, i * 64:i * 64 + 64, :] = inner[:, s * 8:s * 8 + 8].reshape(64, 128).astype(BF16)

    convolve(VG, WB, emit_grad)
    if reduce_here:
        away = pl.multiple_of((1 - core) * 192, 16)
        weight_product(GA, VX, 0, away, 192)
        red_start(0)
        weight_product(GA, VX, 0, top, 192)
        red_first(0)
        wait_faces(2)
        put_halos(2, VH)
        weight_product(GB, VH, 1, away, 192)
        red_start(1)
        red_second(0)
        weight_product(GB, VH, 1, top, 192)
        red_first(1)
        red_third(0)

        def between():
            red_second(1)
            red_fourth(0)

        convolve(VH, WC, emit_out, between)
        red_third(1)
        red_fifth(0)
        red_fourth(1)
        red_end(0)
        for di in range(3):
            turn(F0.at[pl.ds(di * 128, 128)], g1, di * 9)
        red_fifth(1)
        red_end(1)
    else:
        weight_product(GA, VX, 0, 0, 384)
        wait_faces(2)
        put_halos(2, VH)
        weight_product(GB, VH, 1, 0, 384)
        convolve(VH, WC, emit_out)
        g1[...] = R[0]
        F1[...] = R[1]
    for field in range(3):
        drain_faces(field)


def solution(mesh):
    spaces, reps = mesh.shape["space"], mesh.shape["rep"]
    reduce_here = spaces == 8 and reps == 4
    grad_type = BF16 if reduce_here else F32

    def local(voxels, occupied, neighbours, first_weight, second_weight, cotangent):
        smem = pl.BlockSpec(memory_space=pltpu.SMEM)
        vmem = pl.BlockSpec(memory_space=pltpu.VMEM)
        out, first, second = pl.pallas_call(
            functools.partial(kernel, spaces, reps, reduce_here),
            out_shape=(
                jax.ShapeDtypeStruct((4, 512, 128), BF16),
                jax.ShapeDtypeStruct((27, 128, 128) if reduce_here else (384, 1152), grad_type),
                jax.ShapeDtypeStruct((384, 1152), grad_type),
            ),
            in_specs=[smem, smem, vmem, vmem, vmem, vmem],
            out_specs=(vmem, vmem, vmem),
            scratch_shapes=[
                pltpu.VMEM((3, 4, 512, 128), F32),
                pltpu.VMEM((2, 4, 512, 128), F32),
                pltpu.VMEM((6, 8, 64, 128), BF16),
                pltpu.VMEM((6, 8, 64, 128), BF16),
                pltpu.VMEM((6, 8, 64, 128), BF16),
                pltpu.VMEM((10, 10, 32, 384), BF16),
                pltpu.VMEM((10, 10, 32, 384), BF16),
                pltpu.VMEM((10, 10, 32, 384), BF16),
                pltpu.VMEM((4608, 256), BF16),
                pltpu.VMEM((4608, 256), BF16),
                pltpu.VMEM((4608, 256), BF16),
                pltpu.VMEM((8, 256, 128), F32),
                pltpu.VMEM((384, 2560), BF16),
                pltpu.VMEM((384, 2560), BF16),
                pltpu.VMEM((2, 384, 1152), F32),
                pltpu.VMEM((2, 192, 1152), F32),
                pltpu.VMEM((2, 192, 1152), BF16),
                pltpu.VMEM((2, 3, 32, 1152), BF16),
                pltpu.VMEM((2, 3, 32, 384), BF16),
                pltpu.VMEM((2, 32, 1152), F32),
                pltpu.VMEM((2, 32, 1152), BF16),
                pltpu.VMEM((2, 3, 16, 384), BF16),
                pltpu.VMEM((2, 3, 64, 384), BF16),
                pltpu.VMEM((2, 64, 384), F32),
                pltpu.VMEM((2, 64, 384), BF16),
                pltpu.VMEM((384, 1152), grad_type),
                pltpu.SemaphoreType.DMA((3, 6)),
                pltpu.SemaphoreType.DMA((3, 6)),
                pltpu.SemaphoreType.DMA((2, 35)),
                pltpu.SemaphoreType.DMA((2, 35)),
            ],
            compiler_params=pltpu.CompilerParams(
                collective_id=0, has_side_effects=True, vmem_limit_bytes=56 * 2**20
            ),
            cost_estimate=pl.CostEstimate(flops=9_060_000_000, bytes_accessed=6_000_000, transcendentals=500_000),
        )(
            occupied, neighbours, voxels.reshape(4, 512, 128),
            first_weight.reshape(3, 1152, 128), second_weight.reshape(3, 1152, 128),
            cotangent.reshape(4, 512, 128),
        )
        if reduce_here:
            first, second = pl.pallas_call(
                turn_kernel,
                grid=(3,),
                out_shape=[jax.ShapeDtypeStruct((27, 128, 128), F32)] * 2,
                in_specs=[
                    pl.BlockSpec((9, 128, 128), lambda i: (i, 0, 0)),
                    pl.BlockSpec((128, 1152), lambda i: (i, 0)),
                ],
                out_specs=[pl.BlockSpec((9, 128, 128), lambda i: (i, 0, 0))] * 2,
            )(first, second)
            return out[None], first, second
        first, second = lax.psum((first, second), ("space", "rep"))

        def turned(grad):
            return grad.reshape(3, 128, 9, 128).transpose(0, 2, 3, 1).reshape(27, 128, 128)

        return out[None], turned(first), turned(second)

    placed = (
        P("rep", "space", None, None),
        P("rep", "space"),
        P("rep", "space", None),
        P(),
        P(),
        P("rep", "space", None, None),
    )
    return jax.shard_map(
        local,
        mesh=mesh,
        in_specs=placed,
        out_specs=(P("rep", "space", None, None), P(), P()),
        check_vma=False,
    )
```

```python
import functools

import jax
import jax.numpy as jnp
from jax import lax
from jax.experimental import pallas as pl
from jax.experimental.pallas import tpu as pltpu
from jax.sharding import PartitionSpec as P

MESH = pl.DeviceIdType.MESH
OPP = (1, 0, 3, 2, 5, 4)
F32 = jnp.float32
BF16 = jnp.bfloat16


def spread(number, start):
    return [(2 * place + start, place) for place in range(number)]


def eye(size):
    row = lax.broadcasted_iota(jnp.int32, (size, size), 0)
    column = lax.broadcasted_iota(jnp.int32, (size, size), 1)
    return (row == column).astype(F32).astype(BF16)


def last_by_last(left, right):
    return lax.dot_general(left, right, (((1,), (1,)), ((), ())), preferred_element_type=F32)


def turn(source, g, base):
    for m in range(0, 9, 2):
        count = min(2, 9 - m)
        turned = last_by_last(eye(count * 128), source[:, m * 128:(m + count) * 128])
        for n in range(count):
            g[base + m + n] = turned[n * 128:n * 128 + 128].astype(g.dtype)


def turn_kernel(first, second, g1, g2):
    g1[...] = first[...].astype(F32)
    turn(second, g2, 0)


def tile_place(device, spaces):
    plane = spaces.bit_length() - 2
    wide, tall = (plane + 1) // 2, plane // 2
    column = sum(device // 2**src % 2 * 2**dst for src, dst in spread(wide, 0))
    row = sum(device // 2**src % 2 * 2**dst for src, dst in spread(tall, 1))
    layer = device // 2**plane
    return column, row, layer


def tile_owner(column, row, layer, spaces):
    plane = spaces.bit_length() - 2
    wide, tall = (plane + 1) // 2, plane // 2
    owner = layer * 2**plane
    owner = owner + sum(column // 2**dst % 2 * 2**src for src, dst in spread(wide, 0))
    return owner + sum(row // 2**dst % 2 * 2**src for src, dst in spread(tall, 1))


def tile_neighbours(device, spaces):
    plane = spaces.bit_length() - 2
    sizes = (2 ** ((plane + 1) // 2), 2 ** (plane // 2), 2)
    place = tile_place(device, spaces)
    found = []
    for face in range(6):
        dim, step = face // 2, 1 if face % 2 else -1
        moved = list(place)
        moved[dim] = (moved[dim] + step + sizes[dim]) % sizes[dim]
        there = place[dim] < sizes[dim] - 1 if face % 2 else place[dim] > 0
        found.append((there, tile_owner(*moved, spaces)))
    return found


def kernel(
    spaces, reps, reduce_here,
    occ, links, vox, w1, w2, cot,
    out, g1, F1,
    T, U, FB0, FB1, FB2, VX, VH, VG, WA, WB, WC, FI, GA, GB, R, A0, B0, XA, ZA, SA, BA, XB, ZB, SB, BB, F0,
    face_send, face_recv, red_send, red_recv,
):
    FB = (FB0, FB1, FB2)
    space, rep = lax.axis_index("space"), lax.axis_index("rep")
    near = tile_neighbours(space, spaces)
    x, z, y, core = space % 2, space // 2, rep // 2, rep % 2

    def core_peer():
        return (space, y * 2 + (1 - core))

    def xy_peer(d):
        flipped_x = 1 - x if d & 1 else x
        flipped_y = 1 - y if d & 2 else y
        return (z * 2 + flipped_x, flipped_y * 2 + core)

    def z_far(d):
        low = 1 - z % 2 if d & 1 else z % 2
        high = 1 - z // 2 if d & 2 else z // 2
        return high * 2 + low

    def z_peer(d):
        return (z_far(d) * 2 + x, rep)

    barrier = pltpu.get_barrier_semaphore()
    if reduce_here:
        peers = [core_peer()] + [xy_peer(d) for d in (1, 2, 3)] + [z_peer(d) for d in (1, 2, 3)]
        for peer in peers:
            pl.semaphore_signal(barrier, inc=1, device_id=peer, device_id_type=MESH)
        pl.semaphore_wait(barrier, 7)
    else:
        total = 0
        for there, owner in near:
            total = total + there.astype(jnp.int32)

            @pl.when(there)
            def _():
                pl.semaphore_signal(barrier, inc=1, device_id=(owner, rep), device_id_type=MESH)

        pl.semaphore_wait(barrier, total)

    def face_copy(field, face):
        return pltpu.make_async_remote_copy(
            src_ref=FB[field].at[OPP[face], pl.ds(0, 4)],
            dst_ref=FB[field].at[OPP[face], pl.ds(4, 4)],
            send_sem=face_send.at[field, face],
            recv_sem=face_recv.at[field, OPP[face]],
            device_id=(near[face][1], rep),
            device_id_type=MESH,
        )

    def arrival(field, face):
        return pltpu.make_async_remote_copy(
            src_ref=FB[field].at[face, pl.ds(0, 4)],
            dst_ref=FB[field].at[face, pl.ds(4, 4)],
            send_sem=face_send.at[field, face],
            recv_sem=face_recv.at[field, face],
            device_id=(near[face][1], rep),
            device_id_type=MESH,
        )

    def send_faces(field):
        for s in range(4):
            cube = T[field, s].reshape(8, 8, 8, 128)
            parts = (
                cube[0].reshape(64, 128), cube[7].reshape(64, 128),
                cube[:, 0].reshape(64, 128), cube[:, 7].reshape(64, 128),
                T[field, s, pl.ds(0, 64, stride=8), :], T[field, s, pl.ds(7, 64, stride=8), :],
            )
            for face, part in enumerate(parts):
                FB[field][OPP[face], s] = part.astype(BF16)
        for face in (4, 5, 2, 3, 0, 1):
            @pl.when(near[face][0])
            def _():
                face_copy(field, face).start()

    def wait_faces(field):
        for face in range(6):
            @pl.when(near[face][0])
            def _():
                arrival(field, face).wait_recv()

    def drain_faces(field):
        for face in range(6):
            @pl.when(near[face][0])
            def _():
                face_copy(field, face).wait_send()

    def halo(field, face, s):
        link = links[0, s, face]
        there = link >= 0
        safe = jnp.where(there, link, 0)
        index = safe % 4 + jnp.where(safe // 4 == space, 0, 4)
        index = jnp.where(there, index, 0)
        got = FB[field][face, index].astype(F32)
        return jnp.where(there, got, 0.0)

    level = lax.broadcasted_iota(jnp.int32, (1, 8, 128), 1)

    def down(cube):
        return pltpu.roll(cube, 1, 1)

    def up(cube):
        return pltpu.roll(cube, 7, 1)

    def put_centre(field, V):
        def body(i, carry):
            rows = [T[field, s, pl.ds(pl.multiple_of(i * 64, 64), 64), :].reshape(8, 8, 128) for s in range(4)]
            V[i + 1, 1:9, :, 128:256] = jnp.concatenate(rows, axis=1).astype(BF16)
            return carry

        lax.fori_loop(0, 8, body, 0)

    def put_halos(field, V):
        zero = jnp.zeros((32, 384), BF16)
        for i in (0, 9):
            for j in (0, 9):
                V[i, j] = zero
        for s in range(4):
            cube = T[field, s].reshape(64, 8, 128)
            U[0, s] = down(cube).reshape(512, 128)
            U[1, s] = up(cube).reshape(512, 128)
            U[0, s, pl.ds(0, 64, stride=8), :] = halo(field, 4, s)
            U[1, s, pl.ds(7, 64, stride=8), :] = halo(field, 5, s)

        def body(i, carry):
            for n, lane in ((0, 0), (1, 256)):
                rows = [U[n, s, pl.ds(pl.multiple_of(i * 64, 64), 64), :].reshape(8, 8, 128) for s in range(4)]
                V[i + 1, 1:9, :, lane:lane + 128] = jnp.concatenate(rows, axis=1).astype(BF16)
            return carry

        lax.fori_loop(0, 8, body, 0)
        for face in range(4):
            layers = [halo(field, face, s).reshape(8, 8, 128) for s in range(4)]
            lower = [jnp.where(level == 0, 0.0, down(layer)) for layer in layers]
            upper = [jnp.where(level == 7, 0.0, up(layer)) for layer in layers]
            for lane, group in ((0, lower), (128, layers), (256, upper)):
                value = jnp.concatenate(group, axis=1).astype(BF16)
                edge = 9 if face % 2 else 0
                if face < 2:
                    V[edge, 1:9, :, lane:lane + 128] = value
                else:
                    V[1:9, edge, :, lane:lane + 128] = value

    def convolve(V, W, emit, between=None):
        for half in range(2):
            if half and between is not None:
                between()
            groups = []
            for p in range(2):
                base = half * 4 + p * 2
                groups.append(jnp.concatenate(
                    [V[base + a, dj:dj + 8].reshape(256, 384) for a in range(4) for dj in range(3)], axis=1
                ))
            both = jnp.concatenate(groups, axis=0)
            total = jnp.dot(both, W[...], preferred_element_type=F32)
            for p in range(2):
                for h in range(2):
                    emit(half * 4 + p * 2 + h, total[p * 256:p * 256 + 256, h * 128:h * 128 + 128])

    def weight_product(G, V, which, start, count):
        columns = [(dj, dk) for dj in range(3) for dk in range(3)]
        for first in range(0, 9, 2):
            part = columns[first:first + 2]
            right = jnp.concatenate(
                [V[:, dj:dj + 8, :, dk * 128:dk * 128 + 128].reshape(2560, 128) for dj, dk in part], axis=1
            )
            R[which, pl.ds(start, count), first * 128:(first + len(part)) * 128] = jnp.dot(
                G[pl.ds(start, count), :], right, preferred_element_type=F32
            )

    unit = eye(128)

    def put_turned(G, i, rows):
        turned = last_by_last(unit, rows).astype(BF16)
        for di in range(3):
            at = pl.multiple_of((i + di) * 256, 256)
            G[di * 128:di * 128 + 128, pl.ds(at, 256)] = turned

    def clear_turned(G):
        for di in range(3):
            for i in range(10):
                if not 0 <= i - di < 8:
                    G[di * 128:di * 128 + 128, i * 256:i * 256 + 256] = jnp.zeros((128, 256), BF16)

    def widen(W, source):
        blank = jnp.zeros((1152, 128), BF16)
        for a in range(4):
            W[a * 1152:a * 1152 + 1152, 0:128] = source[a] if a < 3 else blank
            W[a * 1152:a * 1152 + 1152, 128:256] = source[a - 1] if a > 0 else blank

    def widen_back(W, source):
        blank = jnp.zeros((1152, 128), BF16)
        W[3456:4608, 0:128] = blank
        W[0:1152, 128:256] = blank
        for a in range(3):
            for t in range(9):
                turned = source[2 - a, (8 - t) * 128:(8 - t) * 128 + 128, :].T
                row = a * 1152 + t * 128
                W[row:row + 128, 0:128] = turned
                W[row + 1152:row + 1280, 128:256] = turned

    def red_copy(which, slot, src, dst, peer):
        return pltpu.make_async_remote_copy(
            src_ref=src, dst_ref=dst, send_sem=red_send.at[which, slot],
            recv_sem=red_recv.at[which, slot], device_id=peer, device_id_type=MESH,
        )

    outs = (F0, F1)
    quarter = y * 2 + x
    D = (1, 2, 3)
    top = pl.multiple_of(core * 192, 16)
    low = pl.multiple_of(core * 192 + 128, 16)
    row_a = pl.multiple_of(core * 192 + quarter * 32, 16)
    row_b = pl.multiple_of(core * 192 + 128 + quarter * 16, 16)

    def quarter_of(d):
        return (1 - y if d & 2 else y) * 2 + (1 - x if d & 1 else x)

    def lanes(place, width):
        return pl.ds(pl.multiple_of(place * 256, 128), width)

    def core_copy(w):
        other = pl.multiple_of((1 - core) * 192, 16)
        return red_copy(w, 0, R.at[w, pl.ds(other, 192)], A0.at[w], core_peer())

    def a_xy(w, d):
        row = pl.multiple_of(quarter_of(d) * 32, 16)
        return red_copy(w, d, B0.at[w, pl.ds(row, 32)], XA.at[w, d - 1], xy_peer(d))

    def a_z(w, d):
        return red_copy(w, 3 + d, BA.at[w, :, lanes(z_far(d), 384)], ZA.at[w, d - 1], z_peer(d))

    def a_back_z(w, d, place):
        ref = outs[w].at[pl.ds(row_a, 32), lanes(place, 256)]
        return red_copy(w, 6 + d, ref, ref, z_peer(d))

    def a_last_z(w, d):
        ref = outs[w].at[pl.ds(row_a, 32), pl.ds(1024, 128)]
        return red_copy(w, 9 + d, ref, ref, z_peer(d))

    def a_back_xy(w, d, q):
        ref = outs[w].at[pl.ds(pl.multiple_of(core * 192 + q * 32, 16), 32)]
        return red_copy(w, 12 + d, ref, ref, xy_peer(d))

    def b_z(w, d):
        return red_copy(w, 15 + d, B0.at[w, pl.ds(128, 64), lanes(z_far(d), 384)], ZB.at[w, d - 1], z_peer(d))

    def b_xy(w, d):
        row = pl.multiple_of(quarter_of(d) * 16, 16)
        return red_copy(w, 18 + d, BB.at[w, pl.ds(row, 16)], XB.at[w, d - 1], xy_peer(d))

    def b_rows(q):
        return pl.ds(pl.multiple_of(core * 192 + 128 + q * 16, 16), 16)

    def b_back_xy(w, d, q):
        ref = outs[w].at[b_rows(q), lanes(z, 256)]
        return red_copy(w, 21 + d, ref, ref, xy_peer(d))

    def b_last_xy(w, d, q):
        ref = outs[w].at[b_rows(q), pl.ds(1024, 128)]
        return red_copy(w, 24 + d, ref, ref, xy_peer(d))

    def b_back_z(w, d, place):
        ref = outs[w].at[pl.ds(low, 64), lanes(place, 256)]
        return red_copy(w, 27 + d, ref, ref, z_peer(d))

    def b_last_z(w, d):
        ref = outs[w].at[pl.ds(low, 64), pl.ds(1024, 128)]
        return red_copy(w, 30 + d, ref, ref, z_peer(d))

    def core_back(w, c):
        ref = outs[w].at[pl.ds(pl.multiple_of(c * 192, 16), 192)]
        return red_copy(w, 34, ref, ref, core_peer())

    def red_start(w):
        core_copy(w).start()

    def red_first(w):
        core_copy(w).wait()
        summed = R[w, pl.ds(top, 192), :] + A0[w]
        R[w, pl.ds(top, 192), :] = summed
        B0[w] = summed.astype(BF16)
        for d in (3, 1, 2):
            a_xy(w, d).start()
            b_z(w, d).start()

    def red_second(w):
        for d in D:
            a_xy(w, d).wait()
        summed = R[w, pl.ds(row_a, 32), :]
        for d in D:
            summed = summed + XA[w, d - 1].astype(F32)
        SA[w] = summed
        BA[w] = summed.astype(BF16)
        for d in (3, 2, 1):
            a_z(w, d).start()
        for d in D:
            b_z(w, d).wait()
        summed = R[w, pl.ds(low, 64), lanes(z, 384)]
        for d in D:
            summed = summed + ZB[w, d - 1].astype(F32)
        SB[w] = summed
        BB[w] = summed.astype(BF16)
        for d in (3, 1, 2):
            b_xy(w, d).start()

    def red_third(w):
        for d in D:
            a_z(w, d).wait()
        summed = SA[w, :, lanes(z, 384)]
        for d in D:
            summed = summed + ZA[w, d - 1].astype(F32)
        whole_a = summed.astype(BF16)
        outs[w][pl.ds(row_a, 32), lanes(z, 256)] = whole_a[:, 0:256]
        for d in (3, 2, 1):
            a_back_z(w, d, z).start()
        for d in D:
            b_xy(w, d).wait()
        summed = SB[w, pl.ds(pl.multiple_of(quarter * 16, 16), 16), :]
        for d in D:
            summed = summed + XB[w, d - 1].astype(F32)
        whole_b = summed.astype(BF16)
        outs[w][pl.ds(row_b, 16), lanes(z, 256)] = whole_b[:, 0:256]
        for d in (3, 1, 2):
            b_back_xy(w, d, quarter).start()

        @pl.when(z == 3)
        def _():
            outs[w][pl.ds(row_a, 32), pl.ds(1024, 128)] = whole_a[:, 256:384]
            outs[w][pl.ds(row_b, 16), pl.ds(1024, 128)] = whole_b[:, 256:384]
            for d in D:
                a_last_z(w, d).start()
                b_last_xy(w, d, quarter).start()

    def red_fourth(w):
        for d in D:
            a_back_z(w, d, z_far(d)).wait_recv()

            @pl.when(z_far(d) == 3)
            def _():
                a_last_z(w, d).wait_recv()
        for d in (3, 1, 2):
            a_back_xy(w, d, quarter).start()
        for d in D:
            b_back_xy(w, d, quarter_of(d)).wait_recv()
        for d in (3, 2, 1):
            b_back_z(w, d, z).start()

        @pl.when(z == 3)
        def _():
            for d in D:
                b_last_xy(w, d, quarter_of(d)).wait_recv()
            for d in D:
                b_last_z(w, d).start()

    def red_fifth(w):
        for d in D:
            a_back_xy(w, d, quarter_of(d)).wait_recv()
            b_back_z(w, d, z_far(d)).wait_recv()

            @pl.when(z_far(d) == 3)
            def _():
                b_last_z(w, d).wait_recv()
        core_back(w, core).start()

    def red_end(w):
        core_back(w, 1 - core).wait_recv()
        core_back(w, core).wait_send()
        for d in D:
            a_back_z(w, d, z).wait_send()
            a_back_xy(w, d, quarter).wait_send()
            b_back_xy(w, d, quarter).wait_send()
            b_back_z(w, d, z).wait_send()

        @pl.when(z == 3)
        def _():
            for d in D:
                a_last_z(w, d).wait_send()
                b_last_xy(w, d, quarter).wait_send()
                b_last_z(w, d).wait_send()

    keep = [occ[0, s].astype(F32) for s in range(4)]
    slot_of = lax.broadcasted_iota(jnp.int32, (32, 128), 0) // 8
    mask = jnp.zeros((32, 128), F32)
    for s in range(4):
        mask = jnp.where(slot_of == s, keep[s], mask)
    mask = mask[None]

    def load(field, source):
        for s in range(4):
            T[field, s] = source[s].astype(F32) * keep[s]

    def masked_rows(rows):
        return (rows.reshape(8, 32, 128) * mask)

    load(0, vox)
    send_faces(0)
    load(1, cot)
    send_faces(1)
    put_centre(0, VX)
    put_centre(1, VG)
    widen(WA, w1)
    clear_turned(GA)
    clear_turned(GB)

    def turn_out(i, carry):
        put_turned(GB, i, VG[i + 1, 1:9, :, 128:256].reshape(256, 128))
        return carry

    lax.fori_loop(0, 8, turn_out, 0)
    wait_faces(0)
    put_halos(0, VX)

    def emit_first(i, rows):
        FI[i] = rows
        hidden = masked_rows(rows * jax.nn.sigmoid(rows))
        for s in range(4):
            T[2, s, i * 64:i * 64 + 64, :] = hidden[:, s * 8:s * 8 + 8].reshape(64, 128)

    convolve(VX, WA, emit_first)
    send_faces(2)
    put_centre(2, VH)
    widen_back(WB, w2)
    widen(WC, w2)
    wait_faces(1)
    put_halos(1, VG)

    def emit_grad(i, rows):
        first = FI[i]
        sigma = jax.nn.sigmoid(first)
        grad = masked_rows(rows * sigma * (1.0 + first * (1.0 - sigma))).reshape(256, 128)
        put_turned(GA, i, grad.astype(BF16))

    def emit_out(i, rows):
        inner = VX[i + 1, 1:9, :, 128:256].astype(F32) + rows.reshape(8, 32, 128)
        inner = (inner * mask).astype(BF16).astype(F32)
        for s in range(4):
            out[s, i * 64:i * 64 + 64, :] = inner[:, s * 8:s * 8 + 8].reshape(64, 128).astype(BF16)

    convolve(VG, WB, emit_grad)
    if reduce_here:
        weight_product(GA, VX, 0, 0, 384)
        red_start(0)
        wait_faces(2)
        put_halos(2, VH)
        red_first(0)
        weight_product(GB, VH, 1, 0, 384)
        red_start(1)
        red_second(0)

        def between():
            red_first(1)
            red_third(0)

        convolve(VH, WC, emit_out, between)
        red_second(1)
        red_fourth(0)
        red_third(1)
        red_fifth(0)
        red_fourth(1)
        red_end(0)
        for di in range(3):
            turn(F0.at[pl.ds(di * 128, 128)], g1, di * 9)
        red_fifth(1)
        red_end(1)
    else:
        weight_product(GA, VX, 0, 0, 384)
        wait_faces(2)
        put_halos(2, VH)
        weight_product(GB, VH, 1, 0, 384)
        convolve(VH, WC, emit_out)
        g1[...] = R[0]
        F1[...] = R[1]
    for field in range(3):
        drain_faces(field)


def solution(mesh):
    spaces, reps = mesh.shape["space"], mesh.shape["rep"]
    reduce_here = spaces == 8 and reps == 4
    grad_type = BF16 if reduce_here else F32

    def local(voxels, occupied, neighbours, first_weight, second_weight, cotangent):
        smem = pl.BlockSpec(memory_space=pltpu.SMEM)
        vmem = pl.BlockSpec(memory_space=pltpu.VMEM)
        out, first, second = pl.pallas_call(
            functools.partial(kernel, spaces, reps, reduce_here),
            out_shape=(
                jax.ShapeDtypeStruct((4, 512, 128), BF16),
                jax.ShapeDtypeStruct((27, 128, 128) if reduce_here else (384, 1152), grad_type),
                jax.ShapeDtypeStruct((384, 1152), grad_type),
            ),
            in_specs=[smem, smem, vmem, vmem, vmem, vmem],
            out_specs=(vmem, vmem, vmem),
            scratch_shapes=[
                pltpu.VMEM((3, 4, 512, 128), F32),
                pltpu.VMEM((2, 4, 512, 128), F32),
                pltpu.VMEM((6, 8, 64, 128), BF16),
                pltpu.VMEM((6, 8, 64, 128), BF16),
                pltpu.VMEM((6, 8, 64, 128), BF16),
                pltpu.VMEM((10, 10, 32, 384), BF16),
                pltpu.VMEM((10, 10, 32, 384), BF16),
                pltpu.VMEM((10, 10, 32, 384), BF16),
                pltpu.VMEM((4608, 256), BF16),
                pltpu.VMEM((4608, 256), BF16),
                pltpu.VMEM((4608, 256), BF16),
                pltpu.VMEM((8, 256, 128), F32),
                pltpu.VMEM((384, 2560), BF16),
                pltpu.VMEM((384, 2560), BF16),
                pltpu.VMEM((2, 384, 1152), F32),
                pltpu.VMEM((2, 192, 1152), F32),
                pltpu.VMEM((2, 192, 1152), BF16),
                pltpu.VMEM((2, 3, 32, 1152), BF16),
                pltpu.VMEM((2, 3, 32, 384), BF16),
                pltpu.VMEM((2, 32, 1152), F32),
                pltpu.VMEM((2, 32, 1152), BF16),
                pltpu.VMEM((2, 3, 16, 384), BF16),
                pltpu.VMEM((2, 3, 64, 384), BF16),
                pltpu.VMEM((2, 64, 384), F32),
                pltpu.VMEM((2, 64, 384), BF16),
                pltpu.VMEM((384, 1152), grad_type),
                pltpu.SemaphoreType.DMA((3, 6)),
                pltpu.SemaphoreType.DMA((3, 6)),
                pltpu.SemaphoreType.DMA((2, 35)),
                pltpu.SemaphoreType.DMA((2, 35)),
            ],
            compiler_params=pltpu.CompilerParams(
                collective_id=0, has_side_effects=True, vmem_limit_bytes=56 * 2**20
            ),
            cost_estimate=pl.CostEstimate(flops=9_060_000_000, bytes_accessed=6_000_000, transcendentals=500_000),
        )(
            occupied, neighbours, voxels.reshape(4, 512, 128),
            first_weight.reshape(3, 1152, 128), second_weight.reshape(3, 1152, 128),
            cotangent.reshape(4, 512, 128),
        )
        if reduce_here:
            first, second = pl.pallas_call(
                turn_kernel,
                grid=(3,),
                out_shape=[jax.ShapeDtypeStruct((27, 128, 128), F32)] * 2,
                in_specs=[
                    pl.BlockSpec((9, 128, 128), lambda i: (i, 0, 0)),
                    pl.BlockSpec((128, 1152), lambda i: (i, 0)),
                ],
                out_specs=[pl.BlockSpec((9, 128, 128), lambda i: (i, 0, 0))] * 2,
            )(first, second)
            return out[None], first, second
        first, second = lax.psum((first, second), ("space", "rep"))

        def turned(grad):
            return grad.reshape(3, 128, 9, 128).transpose(0, 2, 3, 1).reshape(27, 128, 128)

        return out[None], turned(first), turned(second)

    placed = (
        P("rep", "space", None, None),
        P("rep", "space"),
        P("rep", "space", None),
        P(),
        P(),
        P("rep", "space", None, None),
    )
    return jax.shard_map(
        local,
        mesh=mesh,
        in_specs=placed,
        out_specs=(P("rep", "space", None, None), P(), P()),
        check_vma=False,
    )
```
